512 devices in a mesh: ch: 256 (over y, x_lo, z, core), seg: 2 (over x_hi).
Axes of the slice: x: 4 (x_hi: 2, x_lo: 2; x = x_hi * 2 + x_lo), y: 8, z: 8, core: 2. Of those that a mesh axis runs over, the one named last changes fastest.
Arguments:
- spectra: bfloat16 [256, 6, 2, 128, 512], P('ch', 'seg'), may hold values from -6 to 6
- plan: int32 [2, 256], P(None, 'ch'), may hold values from 0 to 255, as said below
Outputs:
- correlations: bfloat16 [256, 2, 128, 128, 128], P('ch', 'seg')
The draws below stay inside these ranges and needn't reach their ends.
Inputs may be any that keep to these rules, and one draw needn't show every extreme that they name: For each round r there is a mask m_r, 1 to 255, with plan[r, b] = b XOR m_r for every block b; the masks of different rounds differ.
All inputs are finite; a program needn't handle non-finite values.
Results may differ from the reference program's by a relative error of at most 0.0055.
Values may be sent and summed in bfloat16 or wider, within the bound.
A program may use at most 64 MiB of HBM per device.

```python
import math
import jax
import jax.numpy as jnp
from jax import lax

CH = 128
BINS = 512
ROUNDS = 2
LAGS = 128
NBLK = 256
SEGMENTS = 6


def draw_plan(key, part):
    key = jax.random.fold_in(key, 7)
    shuffled = jax.random.permutation(key, NBLK - 1).astype(jnp.int32) + 1
    round_masks = shuffled[:ROUNDS]
    block_ids = jnp.arange(NBLK, dtype=jnp.int32)
    return jnp.bitwise_xor(block_ids[None, :], round_masks[:, None]).astype(jnp.int32)


def block_scale(stream_key, shape, cuts, low, top_value):
    factor_of, own = 1.0, jax.random.fold_in(stream_key, 6)
    for dim, parts in cuts:
        draws = jnp.exp(jax.random.uniform(jax.random.fold_in(own, dim), (parts,), jnp.float32, low / len(cuts), top_value / len(cuts)))
        factor_of = factor_of * jnp.repeat(draws, shape[dim] // parts).reshape([-1 if axis == dim else 1 for axis in range(len(shape))])
    return factor_of


def gaussian(stream_key, extent, scale, most, cuts=(), held_as=jnp.bfloat16):
    loudness = block_scale(stream_key, extent, cuts, -0.22, 0.18) if cuts else 1.0
    entries = jax.random.normal(stream_key, extent, jnp.float32) * scale * loudness
    return jnp.minimum(jnp.maximum(entries, -most), most).astype(held_as)


def setup_inputs(seed: int = 0) -> dict:
    keys = jax.random.split(jax.random.key(seed), 3)
    return {
        "spectra": gaussian(keys[0], (NBLK, SEGMENTS, 2, CH, BINS), 1.0, 6.0, ((0, 256), (1, 2))),
        "plan": draw_plan(jax.random.fold_in(keys[2], 71), 0),
    }


def lag_table():
    bin_index = jnp.arange(BINS, dtype=jnp.int32)
    lag_index = jnp.arange(LAGS, dtype=jnp.int32) - LAGS // 2
    product = lag_index[:, None] * bin_index[None, :] % (2 * BINS)
    angles = product.astype(jnp.float32) * (jnp.pi / BINS)
    return jnp.concatenate([jnp.cos(angles), -jnp.sin(angles)], axis=1).astype(jnp.bfloat16)

def block_lags(left_spec, right_spec, table_matrix):
    left_float = left_spec.astype(jnp.float32)
    right_float = right_spec.astype(jnp.float32)
    real_part = jnp.einsum('sif,sjf->fij', left_float[:, 0], right_float[:, 0]) + jnp.einsum('sif,sjf->fij', left_float[:, 1], right_float[:, 1])
    imag_part = jnp.einsum('sif,sjf->fij', left_float[:, 1], right_float[:, 0]) - jnp.einsum('sif,sjf->fij', left_float[:, 0], right_float[:, 1])
    spectrum = jnp.concatenate([real_part, imag_part], axis=0).astype(jnp.bfloat16).reshape(2 * BINS, CH * CH)
    return jnp.dot(table_matrix, spectrum, preferred_element_type=jnp.float32).reshape(LAGS, CH, CH)

def reference(spectra, plan):
    table_matrix = lag_table()
    factor = 1.0 / math.sqrt(2.0 * SEGMENTS * BINS)

    def one_block(block_index):
        mine_block = spectra[block_index]
        results = []
        for round_index in range(ROUNDS):
            partner_block = spectra[plan[round_index, block_index]]
            lags_now = block_lags(mine_block, partner_block, table_matrix)
            results.append((lags_now * factor).astype(jnp.bfloat16))
        return jnp.stack(results)
    return lax.map(one_block, jnp.arange(NBLK, dtype=jnp.int32))
```

```python
import functools
import math

import jax
import jax.numpy as jnp
import numpy as np
from jax import lax
from jax.experimental import pallas as pl
from jax.experimental.pallas import tpu as pltpu
from jax.sharding import PartitionSpec as P

LAGS = 128
MESH = pl.DeviceIdType.MESH
RING = 8
CHUNKS = 8
SLOTS = 2 * CHUNKS + 2
STREAMS = 2
ROWS = 768
PIECE = ROWS // (STREAMS * CHUNKS)


def path(mask, place):
    ahead = ((place ^ mask) - place) % RING
    first = ((place >> 1) & 1) if mask == 5 else 0
    return (0, ahead, first) if ahead <= 4 else (1, RING - ahead, first)


def ring_table():
    table = np.zeros((RING, RING, 16), np.int32)
    for mask in range(RING):
        for place in range(RING):
            row = table[mask, place]
            if mask == 0:
                row[8:10] = 8
            elif mask == 4:
                row[0], row[6], row[8], row[9] = 1, 1, 3, 7
            else:
                direction, _, first = path(mask, place)
                row[direction * 4 + first], row[direction * 4 + first + 2] = 1, 1
                back, hops, start = path(mask, place ^ mask)
                row[8:10] = back * 4 + start + hops - 1
    return table.reshape(-1)


def ring_kernel(plan_ref, table_ref, near_ref, far_ref, out_ref, middle, landed, staged, send_sem, recv_sem):
    ch, seg = lax.axis_index("ch"), lax.axis_index("seg")
    z, y = ch // 2 % RING, ch // 32
    targets = [
        (ch + 32) % 256,
        (ch + 224) % 256,
        ch - z * 2 + (z + 1) % RING * 2,
        ch - z * 2 + (z + RING - 1) % RING * 2,
    ]
    mask = plan_ref[seg, 0] ^ ch
    bases = [(((mask // 32) % RING) * RING + y) * 16, (((mask // 2) % RING) * RING + z) * 16]

    barrier = pltpu.get_barrier_semaphore()
    for target in targets:
        pl.semaphore_signal(barrier, inc=1, device_id=(target, seg), device_id_type=MESH)
    pl.semaphore_wait(barrier, 4)

    halves = (near_ref, far_ref)
    for stage in range(2):
        source = halves if stage == 0 else (middle.at[0], middle.at[1])
        goal = (middle.at[0], middle.at[1]) if stage == 0 else (out_ref.at[0], out_ref.at[1])

        def rows(stream, chunk):
            return pl.ds(pl.multiple_of(stream * (ROWS // STREAMS) + chunk * PIECE, 16), PIECE)

        def copy(link, stream, slot, stage=stage):
            return pltpu.make_async_remote_copy(
                src_ref=staged.at[link, stream, slot % 2],
                dst_ref=landed.at[stage, link, stream, slot],
                send_sem=send_sem.at[link, stream, slot % 2],
                recv_sem=recv_sem.at[stage, link, stream, slot],
                device_id=(targets[link], seg),
                device_id_type=MESH,
            )

        def send(slot, first=False, second=False, stage=stage, source=source):
            for stream in range(STREAMS):
                for dim in range(2):
                    chunk = jnp.minimum(slot // 2, CHUNKS - 1)
                    own = source[dim ^ stage][rows(stream, chunk), :]
                    for direction in range(2):
                        link = 2 * dim + direction
                        value = own
                        if not first:
                            copy(link, stream, slot - 1).wait_recv()
                            if not second:
                                copy(link, stream, slot - 2).wait_send()
                            flag = table_ref[bases[dim] + direction * 4 + slot % 4]
                            value = jnp.where(flag == 1, own, landed[stage, link, stream, slot - 1])
                        staged[link, stream, slot % 2] = value
                        copy(link, stream, slot).start()

        def pick(chunk, stage=stage, source=source, goal=goal):
            for dim in range(2):
                code = table_ref[bases[dim] + 8 + chunk % 2]
                for stream in range(STREAMS):
                    value = source[dim ^ stage][rows(stream, chunk), :]
                    for place in range(8):
                        found = landed[stage, 2 * dim + place // 4, stream, 2 * chunk + place % 4]
                        value = jnp.where(code == place, found, value)
                    goal[dim ^ stage][rows(stream, chunk), :] = value

        send(0, first=True)
        send(1, second=True)

        def pair(number, carry, send=send, pick=pick):
            send(2 * number)

            @pl.when(number >= 2)
            def _():
                pick(number - 2)

            send(2 * number + 1)
            return carry

        lax.fori_loop(1, SLOTS // 2, pair, 0)
        for link in range(4):
            for stream in range(STREAMS):
                copy(link, stream, SLOTS - 1).wait_recv()
                copy(link, stream, SLOTS - 2).wait_send()
                copy(link, stream, SLOTS - 1).wait_send()
        pick(CHUNKS - 1)


def ring_move(plan, near, far):
    width = near.shape[-1]
    vmem = pl.BlockSpec(memory_space=pltpu.VMEM)
    smem = pl.BlockSpec(memory_space=pltpu.SMEM)
    return pl.pallas_call(
        ring_kernel,
        out_shape=jax.ShapeDtypeStruct((2, ROWS, width), jnp.bfloat16),
        in_specs=[smem, smem, vmem, vmem],
        out_specs=vmem,
        scratch_shapes=[
            pltpu.VMEM((2, ROWS, width), jnp.bfloat16),
            pltpu.VMEM((2, 4, STREAMS, SLOTS, PIECE, width), jnp.bfloat16),
            pltpu.VMEM((4, STREAMS, 2, PIECE, width), jnp.bfloat16),
            pltpu.SemaphoreType.DMA((4, STREAMS, 2)),
            pltpu.SemaphoreType.DMA((2, 4, STREAMS, SLOTS)),
        ],
        compiler_params=pltpu.CompilerParams(
            collective_id=0, has_side_effects=True, vmem_limit_bytes=48 * 2**20
        ),
    )(plan, jnp.asarray(ring_table()), near.reshape(ROWS, width), far.reshape(ROWS, width))


def lag_table(bin_count, lag_count):
    bin_index = jnp.arange(bin_count, dtype=jnp.int32)
    lag_index = jnp.arange(lag_count, dtype=jnp.int32) - lag_count // 2
    product = lag_index[:, None] * bin_index[None, :] % (2 * bin_count)
    angles = product.astype(jnp.float32) * (jnp.pi / bin_count)
    return jnp.concatenate([jnp.cos(angles), -jnp.sin(angles)], axis=1).astype(jnp.bfloat16)


def correlate(left_spec, right_spec, table_matrix):
    channels = left_spec.shape[2]
    bin_count = left_spec.shape[3]
    lag_count = table_matrix.shape[0]
    row_block = min(channels, 16)
    right_both = jnp.concatenate([right_spec[:, 0], right_spec[:, 1]], axis=0)

    def one_slab(number, collected):
        first = number * row_block
        row_slab = lax.dynamic_slice_in_dim(left_spec, first, row_block, 2)
        plain_rows = jnp.concatenate([row_slab[:, 0], row_slab[:, 1]], axis=0)
        turned_rows = jnp.concatenate([row_slab[:, 1], -row_slab[:, 0]], axis=0)
        left_both = jnp.concatenate([plain_rows, turned_rows], axis=1)
        both_parts = jnp.einsum(
            "sif,sjf->fij", left_both, right_both, preferred_element_type=jnp.float32
        ).astype(jnp.bfloat16)
        spectrum = jnp.concatenate(
            [both_parts[:, :row_block], both_parts[:, row_block:]], axis=0
        ).reshape(2 * bin_count, row_block * channels)
        lag_part = jnp.dot(table_matrix, spectrum, preferred_element_type=jnp.float32).reshape(
            lag_count, row_block, channels
        )
        return lax.dynamic_update_slice_in_dim(collected, lag_part, first, 1)

    start_value = jnp.zeros((lag_count, channels, channels), jnp.float32)
    return lax.fori_loop(0, channels // row_block, one_slab, start_value)


def swapped(value, bit):
    return lax.ppermute(value, "ch", [(block, block ^ bit) for block in range(lax.axis_size("ch"))])


def per_device(spectra, plan):
    mine = spectra[0]
    seg_dev, bin_count = mine.shape[0], mine.shape[3]
    table_matrix = lag_table(bin_count, LAGS)
    group_count = lax.axis_size("seg")
    factor = 1.0 / math.sqrt(2.0 * seg_dev * group_count * bin_count)
    entry = lax.dynamic_index_in_dim(plan[:, 0], lax.axis_index("seg"), keepdims=False)
    mask = jnp.bitwise_xor(entry, lax.axis_index("ch"))
    others = lax.ppermute(mine, "seg", [(0, 1), (1, 0)])
    left = jnp.concatenate([mine, others], axis=0)
    moved = jnp.where(mask & 16 == 16, swapped(left, 16), left)
    moved = jnp.where(mask & 1 == 1, swapped(moved, 1), moved)
    right = ring_move(plan, moved[:seg_dev], moved[seg_dev:]).reshape(left.shape)
    lags_now = correlate(left, right, table_matrix)
    return (lags_now * factor).astype(jnp.bfloat16)[None, None]


def solution(mesh):
    in_specs = (P("ch", "seg", None, None, None), P(None, "ch"))
    out_specs = P("ch", "seg", None, None, None)
    return jax.shard_map(
        per_device, mesh=mesh, in_specs=in_specs, out_specs=out_specs, check_vma=False
    )
```

```python
import functools
import math

import jax
import jax.numpy as jnp
import numpy as np
from jax import lax
from jax.experimental import pallas as pl
from jax.experimental.pallas import tpu as pltpu
from jax.sharding import PartitionSpec as P

LAGS = 128
MESH = pl.DeviceIdType.MESH
RING = 8
CHUNKS = 4
SLOTS = 2 * CHUNKS + 2
STREAMS = 4
ROWS = 768
PIECE = ROWS // (STREAMS * CHUNKS)


def path(mask, place):
    ahead = ((place ^ mask) - place) % RING
    first = ((place >> 1) & 1) if mask == 5 else 0
    return (0, ahead, first) if ahead <= 4 else (1, RING - ahead, first)


def ring_table():
    table = np.zeros((RING, RING, 16), np.int32)
    for mask in range(RING):
        for place in range(RING):
            row = table[mask, place]
            if mask == 0:
                row[8:10] = 8
            elif mask == 4:
                row[0], row[6], row[8], row[9] = 1, 1, 3, 7
            else:
                direction, _, first = path(mask, place)
                row[direction * 4 + first], row[direction * 4 + first + 2] = 1, 1
                back, hops, start = path(mask, place ^ mask)
                row[8:10] = back * 4 + start + hops - 1
    return table.reshape(-1)


def ring_kernel(plan_ref, table_ref, near_ref, far_ref, out_ref, middle, landed, staged, send_sem, recv_sem):
    ch, seg = lax.axis_index("ch"), lax.axis_index("seg")
    z, y = ch // 2 % RING, ch // 32
    targets = [
        (ch + 32) % 256,
        (ch + 224) % 256,
        ch - z * 2 + (z + 1) % RING * 2,
        ch - z * 2 + (z + RING - 1) % RING * 2,
    ]
    mask = plan_ref[seg, 0] ^ ch
    bases = [(((mask // 32) % RING) * RING + y) * 16, (((mask // 2) % RING) * RING + z) * 16]

    barrier = pltpu.get_barrier_semaphore()
    for target in targets:
        pl.semaphore_signal(barrier, inc=1, device_id=(target, seg), device_id_type=MESH)
    pl.semaphore_wait(barrier, 4)

    halves = (near_ref, far_ref)
    for stage in range(2):
        source = halves if stage == 0 else (middle.at[0], middle.at[1])
        goal = (middle.at[0], middle.at[1]) if stage == 0 else (out_ref.at[0], out_ref.at[1])

        def rows(stream, chunk):
            return pl.ds(pl.multiple_of(stream * (ROWS // STREAMS) + chunk * PIECE, 16), PIECE)

        def copy(link, stream, slot, stage=stage):
            return pltpu.make_async_remote_copy(
                src_ref=staged.at[link, stream, slot % 2],
                dst_ref=landed.at[stage, link, stream, slot],
                send_sem=send_sem.at[link, stream, slot % 2],
                recv_sem=recv_sem.at[stage, link, stream, slot],
                device_id=(targets[link], seg),
                device_id_type=MESH,
            )

        def send(slot, first=False, second=False, stage=stage, source=source):
            for stream in range(STREAMS):
                for dim in range(2):
                    chunk = jnp.minimum(slot // 2, CHUNKS - 1)
                    own = source[dim ^ stage][rows(stream, chunk), :]
                    for direction in range(2):
                        link = 2 * dim + direction
                        value = own
                        if not first:
                            copy(link, stream, slot - 1).wait_recv()
                            if not second:
                                copy(link, stream, slot - 2).wait_send()
                            flag = table_ref[bases[dim] + direction * 4 + slot % 4]
                            value = jnp.where(flag == 1, own, landed[stage, link, stream, slot - 1])
                        staged[link, stream, slot % 2] = value
                        copy(link, stream, slot).start()

        def pick(chunk, stage=stage, source=source, goal=goal):
            for dim in range(2):
                code = table_ref[bases[dim] + 8 + chunk % 2]
                for stream in range(STREAMS):
                    value = source[dim ^ stage][rows(stream, chunk), :]
                    for place in range(8):
                        found = landed[stage, 2 * dim + place // 4, stream, 2 * chunk + place % 4]
                        value = jnp.where(code == place, found, value)
                    goal[dim ^ stage][rows(stream, chunk), :] = value

        send(0, first=True)
        send(1, second=True)

        def pair(number, carry, send=send, pick=pick):
            send(2 * number)

            @pl.when(number >= 2)
            def _():
                pick(number - 2)

            send(2 * number + 1)
            return carry

        lax.fori_loop(1, SLOTS // 2, pair, 0)
        for link in range(4):
            for stream in range(STREAMS):
                copy(link, stream, SLOTS - 1).wait_recv()
                copy(link, stream, SLOTS - 2).wait_send()
                copy(link, stream, SLOTS - 1).wait_send()
        pick(CHUNKS - 1)


def ring_move(plan, near, far):
    width = near.shape[-1]
    vmem = pl.BlockSpec(memory_space=pltpu.VMEM)
    smem = pl.BlockSpec(memory_space=pltpu.SMEM)
    return pl.pallas_call(
        ring_kernel,
        out_shape=jax.ShapeDtypeStruct((2, ROWS, width), jnp.bfloat16),
        in_specs=[smem, smem, vmem, vmem],
        out_specs=vmem,
        scratch_shapes=[
            pltpu.VMEM((2, ROWS, width), jnp.bfloat16),
            pltpu.VMEM((2, 4, STREAMS, SLOTS, PIECE, width), jnp.bfloat16),
            pltpu.VMEM((4, STREAMS, 2, PIECE, width), jnp.bfloat16),
            pltpu.SemaphoreType.DMA((4, STREAMS, 2)),
            pltpu.SemaphoreType.DMA((2, 4, STREAMS, SLOTS)),
        ],
        compiler_params=pltpu.CompilerParams(
            collective_id=0, has_side_effects=True, vmem_limit_bytes=48 * 2**20
        ),
    )(plan, jnp.asarray(ring_table()), near.reshape(ROWS, width), far.reshape(ROWS, width))


BINS = 512
SEGMENTS = 6
CHANNELS = 128
WINDOWS = 8
TONES = 128
SPAN = 2 * TONES


def window_tables():
    time = np.arange(1024)
    bins = np.arange(BINS)
    angle = 2 * np.pi * (np.outer(time, bins) % 1024) / 1024
    weight = np.where(bins == 0, np.sqrt(0.5), 1.0)
    samples = np.concatenate([np.cos(angle) * weight, -np.sin(angle) * weight], axis=1)
    tones = 2 * np.pi * (np.arange(TONES) + 0.5) / SPAN

    def table(offsets):
        turn = np.exp(-1j * np.outer(tones, offsets))
        result = np.empty((TONES, 2, WINDOWS, 2 * BINS))
        for window in range(WINDOWS):
            both = turn @ samples[(window * 128 + offsets) % 1024]
            result[:, 0, window], result[:, 1, window] = both.real, both.imag
        return (result / 32.0).reshape(TONES * 2 * WINDOWS, 2 * BINS)

    return table(np.arange(-64, 192)), table(np.arange(128))


def lag_tables():
    tones = 2 * np.pi * (np.arange(TONES // 2) + 0.5) / SPAN
    scale = 1024.0 / BINS * 2.0 / SPAN / math.sqrt(2.0 * SEGMENTS * BINS)
    even, late, odd = np.arange(0, 65, 2), np.arange(2, 65, 2), np.arange(1, 64, 2)
    parts = [np.cos(np.outer(even, tones)), np.sin(np.outer(late, tones))]
    parts += [np.cos(np.outer(odd, tones)), np.sin(np.outer(odd, tones))]
    return np.kron(np.concatenate(parts, axis=0) * scale, np.eye(8))


def correlate_kernel(left_table, right_table, lag_table, left_near, left_far, right_near, right_far, out_ref,
                     left_turned, right_turned, left_tones, right_tones, folded, constant):
    f32, bf16 = jnp.float32, jnp.bfloat16

    def block(near, far, segment, part):
        source = near if segment < 3 else far
        first = (segment % 3) * 2 * CHANNELS + part * CHANNELS
        return source[first:first + CHANNELS, :]

    for segment in range(SEGMENTS):
        lanes = slice(segment * CHANNELS, (segment + 1) * CHANNELS)
        for part in range(2):
            rows = slice(part * BINS, (part + 1) * BINS)
            left_turned[rows, lanes] = block(left_near, left_far, segment, part).T
            right_turned[rows, lanes] = block(right_near, right_far, segment, part).T

    first_lane = lax.broadcasted_iota(jnp.int32, (CHANNELS, 128), 1) == 0
    total = jnp.zeros((CHANNELS, CHANNELS), f32)
    for segment in range(SEGMENTS):
        mine = jnp.where(first_lane, block(left_near, left_far, segment, 1)[:, :128].astype(f32), 0.0).astype(bf16)
        theirs = block(right_near, right_far, segment, 1)[:, :128]
        total += lax.dot_general(mine, theirs, (((1,), (1,)), ((), ())), preferred_element_type=f32)
    constant[...] = total * (1.0 / math.sqrt(2.0 * SEGMENTS * BINS))

    step = 256

    def tones_of(number, carry):
        rows = pl.ds(pl.multiple_of(number * step, step), step)
        where = pl.ds(number * (step // 16), step // 16)
        left = jnp.dot(left_table[rows, :], left_turned[...], preferred_element_type=f32)
        right = jnp.dot(right_table[rows, :], right_turned[...], preferred_element_type=f32)
        for segment in range(SEGMENTS):
            lanes = slice(segment * CHANNELS, (segment + 1) * CHANNELS)
            depth = slice(segment * 16, (segment + 1) * 16)
            left_tones[where, depth, :] = left[:, lanes].reshape(step // 16, 16, CHANNELS).astype(bf16)
            plain = right[:, lanes].reshape(step // 16, 2, 8, CHANNELS)
            right_tones[where, depth, :CHANNELS] = plain.reshape(step // 16, 16, CHANNELS).astype(bf16)
            turned = jnp.concatenate([-plain[:, 1], plain[:, 0]], axis=1)
            right_tones[where, depth, CHANNELS:] = turned.astype(bf16)
        return carry

    lax.fori_loop(0, TONES * 16 // step, tones_of, 0)

    def cross(tone):
        return jnp.dot(left_tones[tone].T, right_tones[tone], preferred_element_type=f32)

    def fold(number, carry):
        tone = number * 2
        pairs = []
        for offset in range(2):
            low, high = cross(tone + offset), cross(TONES - 1 - tone - offset)
            plus, minus = low + high, low - high
            pairs.append((plus[:, :128], minus[:, 128:], minus[:, :128], plus[:, 128:]))
        rows = pl.ds(pl.multiple_of(number * 16, 16), 16)
        for kind in range(4):
            one, two = pairs[0][kind], pairs[1][kind]
            for group in range(16):
                both = jnp.concatenate([one[group * 8:group * 8 + 8], two[group * 8:group * 8 + 8]], axis=0)
                lanes = slice((group % 2) * 128, (group % 2) * 128 + 128)
                folded[kind, group // 2, rows, lanes] = both.astype(bf16)
        return carry

    lax.fori_loop(0, TONES // 4, fold, 0)

    def lags(pair, carry):
        rows = pl.ds(pl.multiple_of(pair * 16, 16), 16)
        base = constant[rows, :]

        def turn(kind, first, count):
            both = jnp.dot(lag_table[first * 8:(first + count) * 8, :], folded[kind, pair], preferred_element_type=f32)
            both = both.reshape(count, 8, 256)
            return jnp.concatenate([both[:, :, :128], both[:, :, 128:]], axis=1)

        cosines, sines = turn(0, 0, 33) + base, turn(1, 33, 32)
        out_ref[64, rows, :] = cosines[0].astype(bf16)
        for lag in range(1, 33):
            if lag < 32:
                out_ref[64 + 2 * lag, rows, :] = (cosines[lag] - sines[lag - 1]).astype(bf16)
            out_ref[64 - 2 * lag, rows, :] = (cosines[lag] + sines[lag - 1]).astype(bf16)
        cosines, sines = turn(2, 65, 32) + base, turn(3, 97, 32)
        for lag in range(32):
            out_ref[65 + 2 * lag, rows, :] = (cosines[lag] - sines[lag]).astype(bf16)
            out_ref[63 - 2 * lag, rows, :] = (cosines[lag] + sines[lag]).astype(bf16)
        return carry

    lax.fori_loop(0, CHANNELS // 16, lags, 0)


def correlate(left_near, left_far, right_near, right_far):
    tables = [jnp.asarray(table, jnp.bfloat16) for table in (*window_tables(), lag_tables())]
    vmem = pl.BlockSpec(memory_space=pltpu.VMEM)
    bf16 = jnp.bfloat16
    return pl.pallas_call(
        correlate_kernel,
        out_shape=jax.ShapeDtypeStruct((LAGS, CHANNELS, CHANNELS), bf16),
        in_specs=[vmem] * 7,
        out_specs=vmem,
        scratch_shapes=[
            pltpu.VMEM((2 * BINS, SEGMENTS * CHANNELS), bf16),
            pltpu.VMEM((2 * BINS, SEGMENTS * CHANNELS), bf16),
            pltpu.VMEM((TONES, SEGMENTS * 16, CHANNELS), bf16),
            pltpu.VMEM((TONES, SEGMENTS * 16, 2 * CHANNELS), bf16),
            pltpu.VMEM((4, CHANNELS // 16, TONES // 2 * 8, 256), bf16),
            pltpu.VMEM((CHANNELS, CHANNELS), jnp.float32),
        ],
        compiler_params=pltpu.CompilerParams(vmem_limit_bytes=56 * 2**20),
    )(*tables, left_near, left_far, right_near, right_far)


def swapped(value, bit):
    return lax.ppermute(value, "ch", [(block, block ^ bit) for block in range(lax.axis_size("ch"))])


def per_device(spectra, plan):
    mine = spectra[0]
    entry = lax.dynamic_index_in_dim(plan[:, 0], lax.axis_index("seg"), keepdims=False)
    mask = jnp.bitwise_xor(entry, lax.axis_index("ch"))
    others = lax.ppermute(mine, "seg", [(0, 1), (1, 0)])
    moved = jnp.concatenate([mine, others], axis=0)
    moved = jnp.where(mask & 16 == 16, swapped(moved, 16), moved)
    moved = jnp.where(mask & 1 == 1, swapped(moved, 1), moved)
    right = ring_move(plan, moved[:3], moved[3:])
    near, far = mine.reshape(ROWS, BINS), others.reshape(ROWS, BINS)
    return correlate(near, far, right[0], right[1])[None, None]


def solution(mesh):
    in_specs = (P("ch", "seg", None, None, None), P(None, "ch"))
    out_specs = P("ch", "seg", None, None, None)
    return jax.shard_map(
        per_device, mesh=mesh, in_specs=in_specs, out_specs=out_specs, check_vma=False
    )
```

```python
import functools
import math

import jax
import jax.numpy as jnp
import numpy as np
from jax import lax
from jax.experimental import pallas as pl
from jax.experimental.pallas import tpu as pltpu
from jax.sharding import PartitionSpec as P

LAGS = 128
MESH = pl.DeviceIdType.MESH
RING = 8
CHUNKS = 4
SLOTS = 2 * CHUNKS + 2
STREAMS = 4
ROWS = 768
BLOCK = ROWS // CHUNKS
PIECE = BLOCK // STREAMS


def path(mask, place):
    ahead = ((place ^ mask) - place) % RING
    first = ((place >> 1) & 1) if mask == 5 else 0
    return (0, ahead, first) if ahead <= 4 else (1, RING - ahead, first)


def ring_table():
    table = np.zeros((RING, RING, 16), np.int32)
    for mask in range(RING):
        for place in range(RING):
            row = table[mask, place]
            if mask == 0:
                row[8:10] = 8
            elif mask == 4:
                row[0], row[6], row[8], row[9] = 1, 1, 3, 7
            else:
                direction, _, first = path(mask, place)
                row[direction * 4 + first], row[direction * 4 + first + 2] = 1, 1
                back, hops, start = path(mask, place ^ mask)
                row[8:10] = back * 4 + start + hops - 1
    return table.reshape(-1)


def ring_kernel(plan_ref, table_ref, mine_ref, others_ref, near_out, far_out, first, middle, beside, across, opposite,
                chosen, swapped, landed, staged, send_sem, recv_sem, x_send, x_recv):
    ch, seg = lax.axis_index("ch"), lax.axis_index("seg")
    z, y = ch // 2 % RING, ch // 32
    turned = ch + 16 - ch // 16 % 2 * 32
    targets = [
        ((ch + 32) % 256, seg),
        ((ch + 224) % 256, seg),
        (ch - z * 2 + (z + 1) % RING * 2, seg),
        (ch - z * 2 + (z + RING - 1) % RING * 2, seg),
        (turned, seg),
        (turned, 1 - seg),
        (ch + 1 - ch % 2 * 2, seg),
    ]
    mask = plan_ref[seg, 0] ^ ch
    bases = [(((mask // 32) % RING) * RING + y) * 16, (((mask // 2) % RING) * RING + z) * 16]
    x_bit, core_bit = mask // 16 % 2, mask % 2

    barrier = pltpu.get_barrier_semaphore()
    for target in targets:
        pl.semaphore_signal(barrier, inc=1, device_id=target, device_id_type=MESH)
    pl.semaphore_wait(barrier, len(targets))

    def rows(start, count):
        return pl.ds(pl.multiple_of(start, 16), count)

    def x_copy(kind, chunk):
        all_rows = rows(chunk * BLOCK, BLOCK)
        upper, lower = rows(chunk * BLOCK, BLOCK // 2), rows(chunk * BLOCK + BLOCK // 2, BLOCK // 2)
        source, goal, target = [
            (mine_ref.at[all_rows, :], beside.at[all_rows, :], targets[4]),
            (mine_ref.at[all_rows, :], across.at[all_rows, :], targets[5]),
            (beside.at[upper, :], opposite.at[upper, :], targets[5]),
            (across.at[lower, :], opposite.at[lower, :], targets[4]),
            (chosen.at[0, all_rows, :], swapped.at[0, all_rows, :], targets[6]),
            (chosen.at[1, all_rows, :], swapped.at[1, all_rows, :], targets[6]),
        ][kind]
        return pltpu.make_async_remote_copy(
            src_ref=source,
            dst_ref=goal,
            send_sem=x_send.at[kind, chunk],
            recv_sem=x_recv.at[kind, chunk],
            device_id=target,
            device_id_type=MESH,
        )

    def spread(chunk):
        for kind in (0, 1):
            x_copy(kind, chunk).start()

    def forward(chunk):
        for kind in (0, 1):
            x_copy(kind, chunk).wait_recv()
        for kind in (2, 3):
            x_copy(kind, chunk).start()

    def choose(chunk):
        for kind in (2, 3):
            x_copy(kind, chunk).wait_recv()
        here = rows(chunk * BLOCK, BLOCK)
        others_ref[here, :] = opposite[here, :]
        chosen[0, here, :] = jnp.where(x_bit == 1, beside[here, :], mine_ref[here, :])
        chosen[1, here, :] = jnp.where(x_bit == 1, across[here, :], opposite[here, :])
        for kind in (4, 5):
            x_copy(kind, chunk).start()

    def settle(chunk):
        here = rows(chunk * BLOCK, BLOCK)
        for half in range(2):
            x_copy(4 + half, chunk).wait_recv()
            first[half, here, :] = jnp.where(core_bit == 1, swapped[half, here, :], chosen[half, here, :])

    def finish(chunk):
        for kind in range(6):
            x_copy(kind, chunk).wait_send()

    spread(0)
    forward(0)
    spread(1)
    choose(0)
    settle(0)

    for stage in range(2):
        source = (first.at[0], first.at[1]) if stage == 0 else (middle.at[0], middle.at[1])
        goal = (middle.at[0], middle.at[1]) if stage == 0 else (near_out, far_out)

        def piece(stream, chunk):
            return rows(chunk * BLOCK + stream * PIECE, PIECE)

        def copy(link, stream, slot, stage=stage):
            return pltpu.make_async_remote_copy(
                src_ref=staged.at[link, stream, slot % 2],
                dst_ref=landed.at[stage, link, stream, slot],
                send_sem=send_sem.at[link, stream, slot % 2],
                recv_sem=recv_sem.at[stage, link, stream, slot],
                device_id=targets[link],
                device_id_type=MESH,
            )

        def send(slot, first=False, second=False, stage=stage, source=source):
            for stream in range(STREAMS):
                for dim in range(2):
                    chunk = jnp.minimum(slot // 2, CHUNKS - 1)
                    own = source[dim ^ stage][piece(stream, chunk), :]
                    for direction in range(2):
                        link = 2 * dim + direction
                        value = own
                        if not first:
                            copy(link, stream, slot - 1).wait_recv()
                            if not second:
                                copy(link, stream, slot - 2).wait_send()
                            flag = table_ref[bases[dim] + direction * 4 + slot % 4]
                            value = jnp.where(flag == 1, own, landed[stage, link, stream, slot - 1])
                        staged[link, stream, slot % 2] = value
                        copy(link, stream, slot).start()

        def pick(chunk, stage=stage, source=source, goal=goal):
            for dim in range(2):
                code = table_ref[bases[dim] + 8 + chunk % 2]
                for stream in range(STREAMS):
                    value = source[dim ^ stage][piece(stream, chunk), :]
                    for place in range(8):
                        found = landed[stage, 2 * dim + place // 4, stream, 2 * chunk + place % 4]
                        value = jnp.where(code == place, found, value)
                    goal[dim ^ stage][piece(stream, chunk), :] = value

        send(0, first=True)
        if stage == 0:
            forward(1)
        send(1, second=True)
        if stage == 0:
            choose(1)
            spread(2)

        def pair(number, carry, stage=stage, send=send, pick=pick):
            if stage == 0:

                @pl.when(number < CHUNKS)
                def _():
                    settle(number)

            send(2 * number)
            if stage == 0:

                @pl.when(number < CHUNKS - 1)
                def _():
                    forward(number + 1)

            @pl.when(number >= 2)
            def _():
                pick(number - 2)

            send(2 * number + 1)
            if stage == 0:

                @pl.when(number < CHUNKS - 1)
                def _():
                    choose(number + 1)

                @pl.when(number < CHUNKS - 2)
                def _():
                    spread(number + 2)

            return carry

        lax.fori_loop(1, SLOTS // 2, pair, 0)
        for link in range(4):
            for stream in range(STREAMS):
                copy(link, stream, SLOTS - 1).wait_recv()
                copy(link, stream, SLOTS - 2).wait_send()
                copy(link, stream, SLOTS - 1).wait_send()
        pick(CHUNKS - 1)

    for chunk in range(CHUNKS):
        finish(chunk)


def ring_move(plan, mine):
    width = mine.shape[-1]
    vmem = pl.BlockSpec(memory_space=pltpu.VMEM)
    smem = pl.BlockSpec(memory_space=pltpu.SMEM)
    bf16 = jnp.bfloat16
    return pl.pallas_call(
        ring_kernel,
        out_shape=[jax.ShapeDtypeStruct((ROWS, width), bf16)] * 3,
        in_specs=[smem, smem, vmem],
        out_specs=[vmem] * 3,
        scratch_shapes=[
            pltpu.VMEM((2, ROWS, width), bf16),
            pltpu.VMEM((2, ROWS, width), bf16),
            pltpu.VMEM((ROWS, width), bf16),
            pltpu.VMEM((ROWS, width), bf16),
            pltpu.VMEM((ROWS, width), bf16),
            pltpu.VMEM((2, ROWS, width), bf16),
            pltpu.VMEM((2, ROWS, width), bf16),
            pltpu.VMEM((2, 4, STREAMS, SLOTS, PIECE, width), bf16),
            pltpu.VMEM((4, STREAMS, 2, PIECE, width), bf16),
            pltpu.SemaphoreType.DMA((4, STREAMS, 2)),
            pltpu.SemaphoreType.DMA((2, 4, STREAMS, SLOTS)),
            pltpu.SemaphoreType.DMA((6, CHUNKS)),
            pltpu.SemaphoreType.DMA((6, CHUNKS)),
        ],
        compiler_params=pltpu.CompilerParams(
            collective_id=0, has_side_effects=True, vmem_limit_bytes=48 * 2**20
        ),
    )(plan, jnp.asarray(ring_table()), mine)


BINS = 512
SEGMENTS = 6
CHANNELS = 128
WINDOWS = 8
TONES = 128
SPAN = 2 * TONES


def window_tables():
    time = np.arange(1024)
    bins = np.arange(BINS)
    angle = 2 * np.pi * (np.outer(time, bins) % 1024) / 1024
    weight = np.where(bins == 0, np.sqrt(0.5), 1.0)
    samples = np.concatenate([np.cos(angle) * weight, -np.sin(angle) * weight], axis=1)
    tones = 2 * np.pi * (np.arange(TONES) + 0.5) / SPAN

    def table(offsets):
        turn = np.exp(-1j * np.outer(tones, offsets))
        result = np.empty((TONES, 2, WINDOWS, 2 * BINS))
        for window in range(WINDOWS):
            both = turn @ samples[(window * 128 + offsets) % 1024]
            result[:, 0, window], result[:, 1, window] = both.real, both.imag
        return (result / 32.0).reshape(TONES * 2 * WINDOWS, 2 * BINS)

    return table(np.arange(-64, 192)), table(np.arange(128))


def lag_tables():
    tones = 2 * np.pi * (np.arange(TONES // 2) + 0.5) / SPAN
    scale = 1024.0 / BINS * 2.0 / SPAN / math.sqrt(2.0 * SEGMENTS * BINS)
    even, late, odd = np.arange(0, 65, 2), np.arange(2, 65, 2), np.arange(1, 64, 2)
    parts = [np.cos(np.outer(even, tones)), np.sin(np.outer(late, tones))]
    parts += [np.cos(np.outer(odd, tones)), np.sin(np.outer(odd, tones))]
    return np.kron(np.concatenate(parts, axis=0) * scale, np.eye(8))


def correlate_kernel(left_table, right_table, lag_table, left_near, left_far, right_near, right_far, out_ref,
                     left_turned, right_turned, left_tones, right_tones, folded, constant):
    f32, bf16 = jnp.float32, jnp.bfloat16

    def block(near, far, segment, part):
        source = near if segment < 3 else far
        first = (segment % 3) * 2 * CHANNELS + part * CHANNELS
        return source[first:first + CHANNELS, :]

    for segment in range(SEGMENTS):
        lanes = slice(segment * CHANNELS, (segment + 1) * CHANNELS)
        for part in range(2):
            rows = slice(part * BINS, (part + 1) * BINS)
            left_turned[rows, lanes] = block(left_near, left_far, segment, part).T
            right_turned[rows, lanes] = block(right_near, right_far, segment, part).T

    first_lane = lax.broadcasted_iota(jnp.int32, (CHANNELS, 128), 1) == 0
    total = jnp.zeros((CHANNELS, CHANNELS), f32)
    for segment in range(SEGMENTS):
        mine = jnp.where(first_lane, block(left_near, left_far, segment, 1)[:, :128].astype(f32), 0.0).astype(bf16)
        theirs = block(right_near, right_far, segment, 1)[:, :128]
        total += lax.dot_general(mine, theirs, (((1,), (1,)), ((), ())), preferred_element_type=f32)
    constant[...] = total * (1.0 / math.sqrt(2.0 * SEGMENTS * BINS))

    step = 256

    def tones_of(number, carry):
        rows = pl.ds(pl.multiple_of(number * step, step), step)
        where = pl.ds(number * (step // 16), step // 16)
        left = jnp.dot(left_table[rows, :], left_turned[...], preferred_element_type=f32)
        right = jnp.dot(right_table[rows, :], right_turned[...], preferred_element_type=f32)
        for segment in range(SEGMENTS):
            lanes = slice(segment * CHANNELS, (segment + 1) * CHANNELS)
            depth = slice(segment * 16, (segment + 1) * 16)
            left_tones[where, depth, :] = left[:, lanes].reshape(step // 16, 16, CHANNELS).astype(bf16)
            plain = right[:, lanes].reshape(step // 16, 2, 8, CHANNELS)
            right_tones[where, depth, :CHANNELS] = plain.reshape(step // 16, 16, CHANNELS).astype(bf16)
            turned = jnp.concatenate([-plain[:, 1], plain[:, 0]], axis=1)
            right_tones[where, depth, CHANNELS:] = turned.astype(bf16)
        return carry

    lax.fori_loop(0, TONES * 16 // step, tones_of, 0)

    def cross(tone):
        return jnp.dot(left_tones[tone].T, right_tones[tone], preferred_element_type=f32)

    def fold(number, carry):
        tone = number * 2
        pairs = []
        for offset in range(2):
            low, high = cross(tone + offset), cross(TONES - 1 - tone - offset)
            plus, minus = low + high, low - high
            pairs.append((plus[:, :128], minus[:, 128:], minus[:, :128], plus[:, 128:]))
        rows = pl.ds(pl.multiple_of(number * 16, 16), 16)
        for kind in range(4):
            one, two = pairs[0][kind], pairs[1][kind]
            for group in range(16):
                both = jnp.concatenate([one[group * 8:group * 8 + 8], two[group * 8:group * 8 + 8]], axis=0)
                lanes = slice((group % 2) * 128, (group % 2) * 128 + 128)
                folded[kind, group // 2, rows, lanes] = both.astype(bf16)
        return carry

    lax.fori_loop(0, TONES // 4, fold, 0)

    def lags(pair, carry):
        rows = pl.ds(pl.multiple_of(pair * 16, 16), 16)
        base = constant[rows, :]

        def turn(kind, first, count):
            both = jnp.dot(lag_table[first * 8:(first + count) * 8, :], folded[kind, pair], preferred_element_type=f32)
            both = both.reshape(count, 8, 256)
            return jnp.concatenate([both[:, :, :128], both[:, :, 128:]], axis=1)

        cosines, sines = turn(0, 0, 33) + base, turn(1, 33, 32)
        out_ref[64, rows, :] = cosines[0].astype(bf16)
        for lag in range(1, 33):
            if lag < 32:
                out_ref[64 + 2 * lag, rows, :] = (cosines[lag] - sines[lag - 1]).astype(bf16)
            out_ref[64 - 2 * lag, rows, :] = (cosines[lag] + sines[lag - 1]).astype(bf16)
        cosines, sines = turn(2, 65, 32) + base, turn(3, 97, 32)
        for lag in range(32):
            out_ref[65 + 2 * lag, rows, :] = (cosines[lag] - sines[lag]).astype(bf16)
            out_ref[63 - 2 * lag, rows, :] = (cosines[lag] + sines[lag]).astype(bf16)
        return carry

    lax.fori_loop(0, CHANNELS // 16, lags, 0)


def correlate(left_near, left_far, right_near, right_far):
    tables = [jnp.asarray(table, jnp.bfloat16) for table in (*window_tables(), lag_tables())]
    vmem = pl.BlockSpec(memory_space=pltpu.VMEM)
    bf16 = jnp.bfloat16
    return pl.pallas_call(
        correlate_kernel,
        out_shape=jax.ShapeDtypeStruct((LAGS, CHANNELS, CHANNELS), bf16),
        in_specs=[vmem] * 7,
        out_specs=vmem,
        scratch_shapes=[
            pltpu.VMEM((2 * BINS, SEGMENTS * CHANNELS), bf16),
            pltpu.VMEM((2 * BINS, SEGMENTS * CHANNELS), bf16),
            pltpu.VMEM((TONES, SEGMENTS * 16, CHANNELS), bf16),
            pltpu.VMEM((TONES, SEGMENTS * 16, 2 * CHANNELS), bf16),
            pltpu.VMEM((4, CHANNELS // 16, TONES // 2 * 8, 256), bf16),
            pltpu.VMEM((CHANNELS, CHANNELS), jnp.float32),
        ],
        compiler_params=pltpu.CompilerParams(vmem_limit_bytes=56 * 2**20),
    )(*tables, left_near, left_far, right_near, right_far)


def per_device(spectra, plan):
    mine = spectra.reshape(ROWS, BINS)
    others, near, far = ring_move(plan, mine)
    return correlate(mine, others, near, far)[None, None]


def solution(mesh):
    in_specs = (P("ch", "seg", None, None, None), P(None, "ch"))
    out_specs = P("ch", "seg", None, None, None)
    return jax.shard_map(
        per_device, mesh=mesh, in_specs=in_specs, out_specs=out_specs, check_vma=False
    )
```

```python
import functools
import math

import jax
import jax.numpy as jnp
import numpy as np
from jax import lax
from jax.experimental import pallas as pl
from jax.experimental.pallas import tpu as pltpu
from jax.sharding import PartitionSpec as P

LAGS = 128
MESH = pl.DeviceIdType.MESH
RING = 8
CHUNKS = 4
SLOTS = 2 * CHUNKS + 2
STREAMS = 4
ROWS = 768
BLOCK = ROWS // CHUNKS
PIECE = BLOCK // STREAMS


def path(mask, place):
    ahead = ((place ^ mask) - place) % RING
    first = ((place >> 1) & 1) if mask == 5 else 0
    return (0, ahead, first) if ahead <= 4 else (1, RING - ahead, first)


def ring_table():
    table = np.zeros((RING, RING, 16), np.int32)
    for mask in range(RING):
        for place in range(RING):
            row = table[mask, place]
            if mask == 0:
                row[8:10] = 8
            elif mask == 4:
                row[0], row[6], row[8], row[9] = 1, 1, 3, 7
            else:
                direction, _, first = path(mask, place)
                row[direction * 4 + first], row[direction * 4 + first + 2] = 1, 1
                back, hops, start = path(mask, place ^ mask)
                row[8:10] = back * 4 + start + hops - 1
    return table.reshape(-1)
BINS = 512
SEGMENTS = 6
CHANNELS = 128
WINDOWS = 8
TONES = 128
SPAN = 2 * TONES
STEP = 256
PARTS = TONES * 16 // STEP


def sixth(near, far, segment, part):
    first = (segment % 3) * 2 * CHANNELS + part * CHANNELS
    return (near if segment < 3 else far)[first:first + CHANNELS, :]


def lay_out(near, far, turned, segments):
    for segment in segments:
        lanes = slice(segment * CHANNELS, (segment + 1) * CHANNELS)
        for part in range(2):
            turned[part * BINS:(part + 1) * BINS, lanes] = sixth(near, far, segment, part).T


def ring_kernel(plan_ref, table_ref, left_table, mine_ref, tones_out, flat_out, near_out, far_out, first, middle, beside, across,
                opposite, chosen, swapped, landed, staged, left_rows, left_turned, left_tones, flat, send_sem, recv_sem, x_send,
                x_recv, load_sem, store_sem):
    load = pltpu.make_async_copy(left_table, left_rows, load_sem)
    load.start()
    ch, seg = lax.axis_index("ch"), lax.axis_index("seg")
    z, y = ch // 2 % RING, ch // 32
    turned = ch + 16 - ch // 16 % 2 * 32
    targets = [
        ((ch + 32) % 256, seg),
        ((ch + 224) % 256, seg),
        (ch - z * 2 + (z + 1) % RING * 2, seg),
        (ch - z * 2 + (z + RING - 1) % RING * 2, seg),
        (turned, seg),
        (turned, 1 - seg),
        (ch + 1 - ch % 2 * 2, seg),
    ]
    mask = plan_ref[seg, 0] ^ ch
    bases = [(((mask // 32) % RING) * RING + y) * 16, (((mask // 2) % RING) * RING + z) * 16]
    x_bit, core_bit = mask // 16 % 2, mask % 2

    barrier = pltpu.get_barrier_semaphore()
    for target in targets:
        pl.semaphore_signal(barrier, inc=1, device_id=target, device_id_type=MESH)
    pl.semaphore_wait(barrier, len(targets))

    def rows(start, count):
        return pl.ds(pl.multiple_of(start, 16), count)

    def x_copy(kind, chunk):
        all_rows = rows(chunk * BLOCK, BLOCK)
        upper, lower = rows(chunk * BLOCK, BLOCK // 2), rows(chunk * BLOCK + BLOCK // 2, BLOCK // 2)
        source, goal, target = [
            (mine_ref.at[all_rows, :], beside.at[all_rows, :], targets[4]),
            (mine_ref.at[all_rows, :], across.at[all_rows, :], targets[5]),
            (beside.at[upper, :], opposite.at[upper, :], targets[5]),
            (across.at[lower, :], opposite.at[lower, :], targets[4]),
            (chosen.at[0, all_rows, :], swapped.at[0, all_rows, :], targets[6]),
            (chosen.at[1, all_rows, :], swapped.at[1, all_rows, :], targets[6]),
        ][kind]
        return pltpu.make_async_remote_copy(
            src_ref=source,
            dst_ref=goal,
            send_sem=x_send.at[kind, chunk],
            recv_sem=x_recv.at[kind, chunk],
            device_id=target,
            device_id_type=MESH,
        )

    def spread(chunk):
        for kind in (0, 1):
            x_copy(kind, chunk).start()

    def forward(chunk):
        for kind in (0, 1):
            x_copy(kind, chunk).wait_recv()
        for kind in (2, 3):
            x_copy(kind, chunk).start()

    def choose(chunk):
        for kind in (2, 3):
            x_copy(kind, chunk).wait_recv()
        here = rows(chunk * BLOCK, BLOCK)
        chosen[0, here, :] = jnp.where(x_bit == 1, beside[here, :], mine_ref[here, :])
        chosen[1, here, :] = jnp.where(x_bit == 1, across[here, :], opposite[here, :])
        for kind in (4, 5):
            x_copy(kind, chunk).start()

    def settle(chunk):
        here = rows(chunk * BLOCK, BLOCK)
        for half in range(2):
            x_copy(4 + half, chunk).wait_recv()
            first[half, here, :] = jnp.where(core_bit == 1, swapped[half, here, :], chosen[half, here, :])

    def finish(chunk):
        for kind in range(6):
            x_copy(kind, chunk).wait_send()

    def store(number):
        where = pl.ds(number * (STEP // 16), STEP // 16)
        return pltpu.make_async_copy(left_tones.at[where], tones_out.at[where], store_sem.at[number])

    def left_part(number):
        part = rows(number * STEP, STEP)
        tones = jnp.dot(left_rows[part, :], left_turned[...], preferred_element_type=jnp.float32)
        for segment in range(SEGMENTS):
            piece_tones = tones[:, segment * CHANNELS:(segment + 1) * CHANNELS].reshape(STEP // 16, 16, CHANNELS)
            depth = slice(segment * 16, (segment + 1) * 16)
            left_tones[pl.ds(number * (STEP // 16), STEP // 16), depth, :] = piece_tones.astype(jnp.bfloat16)
        store(number).start()

    def flatten():
        first_lane = lax.broadcasted_iota(jnp.int32, (CHANNELS, 128), 1) == 0
        for segment in range(SEGMENTS):
            value = sixth(mine_ref, opposite, segment, 1)[:, :128].astype(jnp.float32)
            flat[segment * CHANNELS:(segment + 1) * CHANNELS, :] = jnp.where(first_lane, value, 0.0).astype(jnp.bfloat16)
        pltpu.make_async_copy(flat, flat_out, store_sem.at[PARTS]).start()

    spread(0)
    forward(0)
    spread(1)
    choose(0)
    settle(0)

    for stage in range(2):
        source = (first.at[0], first.at[1]) if stage == 0 else (middle.at[0], middle.at[1])
        goal = (middle.at[0], middle.at[1]) if stage == 0 else (near_out, far_out)

        def piece(stream, chunk):
            return rows(chunk * BLOCK + stream * PIECE, PIECE)

        def copy(link, stream, slot, stage=stage):
            return pltpu.make_async_remote_copy(
                src_ref=staged.at[link, stream, slot % 2],
                dst_ref=landed.at[stage, link, stream, slot],
                send_sem=send_sem.at[link, stream, slot % 2],
                recv_sem=recv_sem.at[stage, link, stream, slot],
                device_id=targets[link],
                device_id_type=MESH,
            )

        def send(slot, first=False, second=False, stage=stage, source=source):
            for stream in range(STREAMS):
                for dim in range(2):
                    chunk = jnp.minimum(slot // 2, CHUNKS - 1)
                    own = source[dim ^ stage][piece(stream, chunk), :]
                    for direction in range(2):
                        link = 2 * dim + direction
                        value = own
                        if not first:
                            copy(link, stream, slot - 1).wait_recv()
                            if not second:
                                copy(link, stream, slot - 2).wait_send()
                            flag = table_ref[bases[dim] + direction * 4 + slot % 4]
                            value = jnp.where(flag == 1, own, landed[stage, link, stream, slot - 1])
                        staged[link, stream, slot % 2] = value
                        copy(link, stream, slot).start()

        def pick(chunk, stage=stage, source=source, goal=goal):
            for dim in range(2):
                code = table_ref[bases[dim] + 8 + chunk % 2]
                for stream in range(STREAMS):
                    value = source[dim ^ stage][piece(stream, chunk), :]
                    for place in range(8):
                        found = landed[stage, 2 * dim + place // 4, stream, 2 * chunk + place % 4]
                        value = jnp.where(code == place, found, value)
                    goal[dim ^ stage][piece(stream, chunk), :] = value

        send(0, first=True)
        if stage == 0:
            forward(1)
        else:
            lay_out(mine_ref, opposite, left_turned, range(3))
        send(1, second=True)
        if stage == 0:
            choose(1)
            spread(2)
        else:
            lay_out(mine_ref, opposite, left_turned, range(3, 6))
            flatten()
            load.wait()

        def pair(number, carry, stage=stage, send=send, pick=pick):
            if stage == 0:

                @pl.when(number < CHUNKS)
                def _():
                    settle(number)

            send(2 * number)
            if stage == 0:

                @pl.when(number < CHUNKS - 1)
                def _():
                    forward(number + 1)

            else:
                left_part(2 * number - 2)

            @pl.when(number >= 2)
            def _():
                pick(number - 2)

            send(2 * number + 1)
            if stage == 0:

                @pl.when(number < CHUNKS - 1)
                def _():
                    choose(number + 1)

                @pl.when(number < CHUNKS - 2)
                def _():
                    spread(number + 2)

            else:
                left_part(2 * number - 1)

            return carry

        lax.fori_loop(1, SLOTS // 2, pair, 0)
        for link in range(4):
            for stream in range(STREAMS):
                copy(link, stream, SLOTS - 1).wait_recv()
                copy(link, stream, SLOTS - 2).wait_send()
                copy(link, stream, SLOTS - 1).wait_send()
        pick(CHUNKS - 1)

    for chunk in range(CHUNKS):
        finish(chunk)
    for number in range(PARTS):
        store(number).wait()
    pltpu.make_async_copy(flat, flat_out, store_sem.at[PARTS]).wait()


def ring_move(plan, mine, left_table):
    width = mine.shape[-1]
    vmem = pl.BlockSpec(memory_space=pltpu.VMEM)
    smem = pl.BlockSpec(memory_space=pltpu.SMEM)
    hbm = pl.BlockSpec(memory_space=pl.ANY)
    bf16 = jnp.bfloat16
    return pl.pallas_call(
        ring_kernel,
        out_shape=[
            jax.ShapeDtypeStruct((TONES, SEGMENTS * 16, CHANNELS), bf16),
            jax.ShapeDtypeStruct((SEGMENTS * CHANNELS, 128), bf16),
            jax.ShapeDtypeStruct((ROWS, width), bf16),
            jax.ShapeDtypeStruct((ROWS, width), bf16),
        ],
        in_specs=[smem, smem, hbm, vmem],
        out_specs=[hbm, hbm, vmem, vmem],
        scratch_shapes=[
            pltpu.VMEM((2, ROWS, width), bf16),
            pltpu.VMEM((2, ROWS, width), bf16),
            pltpu.VMEM((ROWS, width), bf16),
            pltpu.VMEM((ROWS, width), bf16),
            pltpu.VMEM((ROWS, width), bf16),
            pltpu.VMEM((2, ROWS, width), bf16),
            pltpu.VMEM((2, ROWS, width), bf16),
            pltpu.VMEM((2, 4, STREAMS, SLOTS, PIECE, width), bf16),
            pltpu.VMEM((4, STREAMS, 2, PIECE, width), bf16),
            pltpu.VMEM((TONES * 16, 2 * BINS), bf16),
            pltpu.VMEM((2 * BINS, SEGMENTS * CHANNELS), bf16),
            pltpu.VMEM((TONES, SEGMENTS * 16, CHANNELS), bf16),
            pltpu.VMEM((SEGMENTS * CHANNELS, 128), bf16),
            pltpu.SemaphoreType.DMA((4, STREAMS, 2)),
            pltpu.SemaphoreType.DMA((2, 4, STREAMS, SLOTS)),
            pltpu.SemaphoreType.DMA((6, CHUNKS)),
            pltpu.SemaphoreType.DMA((6, CHUNKS)),
            pltpu.SemaphoreType.DMA,
            pltpu.SemaphoreType.DMA((PARTS + 1,)),
        ],
        compiler_params=pltpu.CompilerParams(
            collective_id=0, has_side_effects=True, vmem_limit_bytes=56 * 2**20
        ),
    )(plan, jnp.asarray(ring_table()), left_table, mine)


def window_tables():
    time = np.arange(1024)
    bins = np.arange(BINS)
    angle = 2 * np.pi * (np.outer(time, bins) % 1024) / 1024
    weight = np.where(bins == 0, np.sqrt(0.5), 1.0)
    samples = np.concatenate([np.cos(angle) * weight, -np.sin(angle) * weight], axis=1)
    tones = 2 * np.pi * (np.arange(TONES) + 0.5) / SPAN

    def table(offsets):
        turn = np.exp(-1j * np.outer(tones, offsets))
        result = np.empty((TONES, 2, WINDOWS, 2 * BINS))
        for window in range(WINDOWS):
            both = turn @ samples[(window * 128 + offsets) % 1024]
            result[:, 0, window], result[:, 1, window] = both.real, both.imag
        return (result / 32.0).reshape(TONES * 2 * WINDOWS, 2 * BINS)

    return table(np.arange(-64, 192)), table(np.arange(128))


def lag_tables():
    tones = 2 * np.pi * (np.arange(TONES // 2) + 0.5) / SPAN
    scale = 1024.0 / BINS * 2.0 / SPAN / math.sqrt(2.0 * SEGMENTS * BINS)
    even, late, odd = np.arange(0, 65, 2), np.arange(2, 65, 2), np.arange(1, 64, 2)
    parts = [np.cos(np.outer(even, tones)), np.sin(np.outer(late, tones))]
    parts += [np.cos(np.outer(odd, tones)), np.sin(np.outer(odd, tones))]
    return np.kron(np.concatenate(parts, axis=0) * scale, np.eye(8))


def correlate_kernel(right_table, lag_table, left_ref, flat_ref, near_ref, far_ref, out_ref,
                     right_rows, lag_rows, left_tones, flat, near, far, right_turned, right_tones, folded, constant, held,
                     load_sem, part_sem, out_sem):
    f32, bf16 = jnp.float32, jnp.bfloat16
    loads = [
        pltpu.make_async_copy(source, goal, load_sem.at[number])
        for number, (source, goal) in enumerate(
            [(near_ref, near), (far_ref, far), (flat_ref, flat), (left_ref, left_tones), (lag_table, lag_rows)]
        )
    ]

    def part_rows(number):
        return pl.ds(pl.multiple_of(number * STEP, STEP), STEP)

    def part_load(number):
        rows = part_rows(number)
        return pltpu.make_async_copy(right_table.at[rows, :], right_rows.at[rows, :], part_sem.at[number])

    def result(pair):
        rows = pl.ds(pl.multiple_of(pair * 16, 16), 16)
        return pltpu.make_async_copy(held.at[pair % 2], out_ref.at[:, rows, :], out_sem.at[pair % 2])

    for load in loads[:2]:
        load.start()
    for number in range(PARTS):
        part_load(number).start()
    for load in loads[2:]:
        load.start()

    loads[0].wait()
    lay_out(near, far, right_turned, range(3))
    loads[1].wait()
    lay_out(near, far, right_turned, range(3, 6))

    def tones_of(number, carry):
        part_load(number).wait()
        where = pl.ds(number * (STEP // 16), STEP // 16)
        right = jnp.dot(right_rows[part_rows(number), :], right_turned[...], preferred_element_type=f32)
        for segment in range(SEGMENTS):
            lanes = slice(segment * CHANNELS, (segment + 1) * CHANNELS)
            depth = slice(segment * 16, (segment + 1) * 16)
            plain = right[:, lanes].reshape(STEP // 16, 2, 8, CHANNELS)
            right_tones[where, depth, :CHANNELS] = plain.reshape(STEP // 16, 16, CHANNELS).astype(bf16)
            turned = jnp.concatenate([-plain[:, 1], plain[:, 0]], axis=1)
            right_tones[where, depth, CHANNELS:] = turned.astype(bf16)
        return carry

    lax.fori_loop(0, PARTS, tones_of, 0)

    loads[2].wait()
    total = jnp.zeros((CHANNELS, CHANNELS), f32)
    for segment in range(SEGMENTS):
        mine = flat[segment * CHANNELS:(segment + 1) * CHANNELS, :]
        theirs = sixth(near, far, segment, 1)[:, :128]
        total += lax.dot_general(mine, theirs, (((1,), (1,)), ((), ())), preferred_element_type=f32)
    constant[...] = total * (1.0 / math.sqrt(2.0 * SEGMENTS * BINS))
    loads[3].wait()

    def cross(tone):
        return jnp.dot(left_tones[tone].T, right_tones[tone], preferred_element_type=f32)

    def fold(number, carry):
        tone = number * 2
        pairs = []
        for offset in range(2):
            low, high = cross(tone + offset), cross(TONES - 1 - tone - offset)
            plus, minus = low + high, low - high
            pairs.append((plus[:, :128], minus[:, 128:], minus[:, :128], plus[:, 128:]))
        rows = pl.ds(pl.multiple_of(number * 16, 16), 16)
        for kind in range(4):
            one, two = pairs[0][kind], pairs[1][kind]
            for group in range(16):
                both = jnp.concatenate([one[group * 8:group * 8 + 8], two[group * 8:group * 8 + 8]], axis=0)
                lanes = slice((group % 2) * 128, (group % 2) * 128 + 128)
                folded[kind, group // 2, rows, lanes] = both.astype(bf16)
        return carry

    lax.fori_loop(0, TONES // 4, fold, 0)
    loads[4].wait()

    def lags(pair, carry):
        slot = pair % 2
        base = constant[pl.ds(pl.multiple_of(pair * 16, 16), 16), :]

        @pl.when(pair >= 2)
        def _():
            result(pair - 2).wait()

        def turn(kind, first, count):
            both = jnp.dot(lag_rows[first * 8:(first + count) * 8, :], folded[kind, pair], preferred_element_type=f32)
            both = both.reshape(count, 8, 256)
            return jnp.concatenate([both[:, :, :128], both[:, :, 128:]], axis=1)

        cosines, sines = turn(0, 0, 33) + base, turn(1, 33, 32)
        held[slot, 64, :, :] = cosines[0].astype(bf16)
        for lag in range(1, 33):
            if lag < 32:
                held[slot, 64 + 2 * lag, :, :] = (cosines[lag] - sines[lag - 1]).astype(bf16)
            held[slot, 64 - 2 * lag, :, :] = (cosines[lag] + sines[lag - 1]).astype(bf16)
        cosines, sines = turn(2, 65, 32) + base, turn(3, 97, 32)
        for lag in range(32):
            held[slot, 65 + 2 * lag, :, :] = (cosines[lag] - sines[lag]).astype(bf16)
            held[slot, 63 - 2 * lag, :, :] = (cosines[lag] + sines[lag]).astype(bf16)
        result(pair).start()
        return carry

    lax.fori_loop(0, CHANNELS // 16, lags, 0)
    result(CHANNELS // 16 - 2).wait()
    result(CHANNELS // 16 - 1).wait()


def correlate(left_tones, flat, near, far, right_table, lag_table):
    hbm = pl.BlockSpec(memory_space=pl.ANY)
    bf16 = jnp.bfloat16
    return pl.pallas_call(
        correlate_kernel,
        out_shape=jax.ShapeDtypeStruct((LAGS, CHANNELS, CHANNELS), bf16),
        in_specs=[hbm] * 6,
        out_specs=hbm,
        scratch_shapes=[
            pltpu.VMEM(right_table.shape, bf16),
            pltpu.VMEM(lag_table.shape, bf16),
            pltpu.VMEM(left_tones.shape, bf16),
            pltpu.VMEM(flat.shape, bf16),
            pltpu.VMEM(near.shape, bf16),
            pltpu.VMEM(far.shape, bf16),
            pltpu.VMEM((2 * BINS, SEGMENTS * CHANNELS), bf16),
            pltpu.VMEM((TONES, SEGMENTS * 16, 2 * CHANNELS), bf16),
            pltpu.VMEM((4, CHANNELS // 16, TONES // 2 * 8, 256), bf16),
            pltpu.VMEM((CHANNELS, CHANNELS), jnp.float32),
            pltpu.VMEM((2, LAGS, 16, CHANNELS), bf16),
            pltpu.SemaphoreType.DMA((5,)),
            pltpu.SemaphoreType.DMA((PARTS,)),
            pltpu.SemaphoreType.DMA((2,)),
        ],
        compiler_params=pltpu.CompilerParams(vmem_limit_bytes=56 * 2**20),
    )(right_table, lag_table, left_tones, flat, near, far)


def per_device(spectra, plan):
    left_table, right_table = (jnp.asarray(table, jnp.bfloat16) for table in window_tables())
    lag_table = jnp.asarray(lag_tables(), jnp.bfloat16)
    left_tones, flat, near, far = ring_move(plan, spectra.reshape(ROWS, BINS), left_table)
    return correlate(left_tones, flat, near, far, right_table, lag_table)[None, None]


def solution(mesh):
    in_specs = (P("ch", "seg", None, None, None), P(None, "ch"))
    out_specs = P("ch", "seg", None, None, None)
    return jax.shard_map(
        per_device, mesh=mesh, in_specs=in_specs, out_specs=out_specs, check_vma=False
    )
```

```python
import functools
import math

import jax
import jax.numpy as jnp
import numpy as np
from jax import lax
from jax.experimental import pallas as pl
from jax.experimental.pallas import tpu as pltpu
from jax.sharding import PartitionSpec as P

LAGS = 128
MESH = pl.DeviceIdType.MESH
RING = 8
CHUNKS = 4
SLOTS = 2 * CHUNKS
WIDTH = 2 * SLOTS + CHUNKS
STREAMS = 4
ROWS = 768
BLOCK = ROWS // CHUNKS
PIECE = BLOCK // STREAMS


def ring_plan():
    sends, lands = {}, {}

    def travel(mask, place, direction, chunk, slots):
        for hop, slot in enumerate(slots):
            at = (mask, (place + (hop if direction == 0 else -hop)) % RING, slot, direction)
            assert at not in sends and slot < SLOTS
            sends[at] = ("own", chunk) if hop == 0 else ("pass", slots[hop - 1])
        lands[mask, place ^ mask, chunk] = (direction, slots[-1])

    for mask in range(1, RING):
        for place in range(RING):
            ahead = ((place ^ mask) - place) % RING
            direction, hops = (0, ahead) if ahead <= 4 else (1, RING - ahead)
            for chunk in range(CHUNKS):
                if mask == 4:
                    travel(mask, place, chunk % 2, chunk, [4 * (chunk // 2) + hop for hop in range(4)])
                elif mask in (3, 7):
                    slots = [chunk, chunk + 1, chunk + 2] if hops == 3 else [CHUNKS + chunk if chunk else 0]
                    travel(mask, place, direction, chunk, slots)
                else:
                    slots = [[chunk], [chunk, CHUNKS + chunk], [chunk, chunk + 1, CHUNKS + chunk]][hops - 1]
                    travel(mask, place, direction, chunk, slots)

    sources = [
        [sorted({what for at, what in sends.items() if at[2:] == (slot, way)}) for way in range(2)] for slot in range(SLOTS)
    ]
    spots = [sorted({where for at, where in lands.items() if at[2] == chunk}) + [None] for chunk in range(CHUNKS)]
    table = np.zeros((RING, RING, WIDTH), np.int32)
    for (mask, place, slot, way), what in sends.items():
        table[mask, place, slot * 2 + way] = sources[slot][way].index(what)
    for chunk in range(CHUNKS):
        for mask in range(RING):
            for place in range(RING):
                table[mask, place, 2 * SLOTS + chunk] = spots[chunk].index(lands.get((mask, place, chunk)))
    return sources, spots, table.reshape(-1)


SOURCES, SPOTS, CODES = ring_plan()
BINS = 512
SEGMENTS = 6
CHANNELS = 128
WINDOWS = 8
TONES = 128
SPAN = 2 * TONES
STEP = 256
UNROLL = 8
PARTS = TONES * 16 // STEP


def sixth(near, far, segment, part):
    first = (segment % 3) * 2 * CHANNELS + part * CHANNELS
    return (near if segment < 3 else far)[first:first + CHANNELS, :]


def lay_out(near, far, turned, segments):
    for segment in segments:
        lanes = slice(segment * CHANNELS, (segment + 1) * CHANNELS)
        for part in range(2):
            turned[part * BINS:(part + 1) * BINS, lanes] = sixth(near, far, segment, part).T


def ring_kernel(plan_ref, table_ref, left_table, mine_ref, tones_out, flat_out, near_out, far_out, first, middle, beside, across,
                opposite, chosen, swapped, landed, staged, left_rows, left_turned, left_tones, flat, send_sem, recv_sem, x_send,
                x_recv, load_sem, store_sem):
    load = pltpu.make_async_copy(left_table, left_rows, load_sem)
    load.start()
    ch, seg = lax.axis_index("ch"), lax.axis_index("seg")
    z, y = ch // 2 % RING, ch // 32
    turned = ch + 16 - ch // 16 % 2 * 32
    targets = [
        ((ch + 32) % 256, seg),
        ((ch + 224) % 256, seg),
        (ch - z * 2 + (z + 1) % RING * 2, seg),
        (ch - z * 2 + (z + RING - 1) % RING * 2, seg),
        (turned, seg),
        (turned, 1 - seg),
        (ch + 1 - ch % 2 * 2, seg),
    ]
    mask = plan_ref[seg, 0] ^ ch
    bases = [(((mask // 32) % RING) * RING + y) * WIDTH, (((mask // 2) % RING) * RING + z) * WIDTH]
    x_bit, core_bit = mask // 16 % 2, mask % 2

    barrier = pltpu.get_barrier_semaphore()
    for target in targets:
        pl.semaphore_signal(barrier, inc=1, device_id=target, device_id_type=MESH)
    pl.semaphore_wait(barrier, len(targets))

    def rows(start, count):
        return pl.ds(pl.multiple_of(start, 16), count)

    def x_copy(kind, chunk):
        all_rows = rows(chunk * BLOCK, BLOCK)
        upper, lower = rows(chunk * BLOCK, BLOCK // 2), rows(chunk * BLOCK + BLOCK // 2, BLOCK // 2)
        source, goal, target = [
            (mine_ref.at[all_rows, :], beside.at[all_rows, :], targets[4]),
            (mine_ref.at[all_rows, :], across.at[all_rows, :], targets[5]),
            (beside.at[upper, :], opposite.at[upper, :], targets[5]),
            (across.at[lower, :], opposite.at[lower, :], targets[4]),
            (chosen.at[0, all_rows, :], swapped.at[0, all_rows, :], targets[6]),
            (chosen.at[1, all_rows, :], swapped.at[1, all_rows, :], targets[6]),
        ][kind]
        return pltpu.make_async_remote_copy(
            src_ref=source,
            dst_ref=goal,
            send_sem=x_send.at[kind, chunk],
            recv_sem=x_recv.at[kind, chunk],
            device_id=target,
            device_id_type=MESH,
        )

    def spread(chunk):
        for kind in (0, 1):
            x_copy(kind, chunk).start()

    def forward(chunk):
        for kind in (0, 1):
            x_copy(kind, chunk).wait_recv()
        for kind in (2, 3):
            x_copy(kind, chunk).start()

    def choose(chunk):
        for kind in (2, 3):
            x_copy(kind, chunk).wait_recv()
        here = rows(chunk * BLOCK, BLOCK)
        chosen[0, here, :] = jnp.where(x_bit == 1, beside[here, :], mine_ref[here, :])
        chosen[1, here, :] = jnp.where(x_bit == 1, across[here, :], opposite[here, :])
        for kind in (4, 5):
            x_copy(kind, chunk).start()

    def settle(chunk):
        here = rows(chunk * BLOCK, BLOCK)
        for half in range(2):
            x_copy(4 + half, chunk).wait_recv()
            first[half, here, :] = jnp.where(core_bit == 1, swapped[half, here, :], chosen[half, here, :])

    def finish(chunk):
        for kind in range(6):
            x_copy(kind, chunk).wait_send()

    def store(number):
        where = pl.ds(number * (STEP // 16), STEP // 16)
        return pltpu.make_async_copy(left_tones.at[where], tones_out.at[where], store_sem.at[number])

    def left_part(number):
        part = rows(number * STEP, STEP)
        tones = jnp.dot(left_rows[part, :], left_turned[...], preferred_element_type=jnp.float32)
        for segment in range(SEGMENTS):
            piece_tones = tones[:, segment * CHANNELS:(segment + 1) * CHANNELS].reshape(STEP // 16, 16, CHANNELS)
            depth = slice(segment * 16, (segment + 1) * 16)
            left_tones[pl.ds(number * (STEP // 16), STEP // 16), depth, :] = piece_tones.astype(jnp.bfloat16)
        store(number).start()

    def flatten():
        first_lane = lax.broadcasted_iota(jnp.int32, (CHANNELS, 128), 1) == 0
        for segment in range(SEGMENTS):
            value = sixth(mine_ref, opposite, segment, 1)[:, :128].astype(jnp.float32)
            flat[segment * CHANNELS:(segment + 1) * CHANNELS, :] = jnp.where(first_lane, value, 0.0).astype(jnp.bfloat16)
        pltpu.make_async_copy(flat, flat_out, store_sem.at[PARTS]).start()

    spread(0)
    forward(0)
    spread(1)
    choose(0)
    forward(1)
    spread(2)
    settle(0)
    choose(1)
    settle(1)

    def beside_slot(stage, slot):
        if stage == 0:
            if slot == 0:
                forward(2)
                spread(3)
            elif slot == 1:
                forward(3)
                choose(2)
                settle(2)
            elif slot == 2:
                choose(3)
                settle(3)
            elif slot == 3:
                lay_out(mine_ref, opposite, left_turned, range(3))
            elif slot == 4:
                lay_out(mine_ref, opposite, left_turned, range(3, 6))
                flatten()
            elif slot == 5:
                load.wait()
            if slot >= 6:
                left_part(slot - 6)
        elif slot < 6:
            left_part(slot + 2)

    def ring_copy(stage, link, stream, slot):
        return pltpu.make_async_remote_copy(
            src_ref=staged.at[link, stream, slot % 2],
            dst_ref=landed.at[stage, link, stream, slot],
            send_sem=send_sem.at[link, stream, slot % 2],
            recv_sem=recv_sem.at[stage, link, stream, slot],
            device_id=targets[link],
            device_id_type=MESH,
        )

    def piece(stream, chunk):
        return rows(chunk * BLOCK + stream * PIECE, PIECE)

    def each_stream(body):
        def step(stream, carry):
            body(stream)
            return carry

        lax.fori_loop(0, STREAMS, step, 0)

    def send(stage, slot, source):
        def one(stream):
            for dim in range(2):
                for way in range(2):
                    link = 2 * dim + way
                    if slot >= 1:
                        ring_copy(stage, link, stream, slot - 1).wait_recv()
                    if slot >= 2:
                        ring_copy(stage, link, stream, slot - 2).wait_send()
                    code = table_ref[bases[dim] + slot * 2 + way]
                    value = None
                    for number, (kind, index) in enumerate(SOURCES[slot][way]):
                        if kind == "own":
                            option = source[dim ^ stage][piece(stream, index), :]
                        else:
                            option = landed[stage, link, stream, index]
                        value = option if value is None else jnp.where(code == number, option, value)
                    staged[link, stream, slot % 2] = value
                    ring_copy(stage, link, stream, slot).start()

        each_stream(one)

    def pick(stage, chunk, source, goal):
        def one(stream):
            for dim in range(2):
                code = table_ref[bases[dim] + 2 * SLOTS + chunk]
                value = source[dim ^ stage][piece(stream, chunk), :]
                for number, spot in enumerate(SPOTS[chunk][:-1]):
                    value = jnp.where(code == number, landed[stage, 2 * dim + spot[0], stream, spot[1]], value)
                goal[dim ^ stage][piece(stream, chunk), :] = value

        each_stream(one)

    def drain(stage):
        def one(stream):
            for link in range(4):
                ring_copy(stage, link, stream, SLOTS - 1).wait_recv()
                ring_copy(stage, link, stream, SLOTS - 2).wait_send()
                ring_copy(stage, link, stream, SLOTS - 1).wait_send()

        each_stream(one)

    last = [max(spot[1] for spot in spots[:-1]) for spots in SPOTS]
    sides = [(first.at[0], first.at[1]), (middle.at[0], middle.at[1]), (near_out, far_out)]
    late = []
    for stage in range(2):
        source, goal = sides[stage], sides[stage + 1]
        for slot in range(SLOTS):
            send(stage, slot, source)
            for chunk in late:
                pick(0, chunk, sides[0], sides[1])
            late = []
            for chunk in range(CHUNKS):
                if last[chunk] == slot - 1:
                    pick(stage, chunk, source, goal)
            beside_slot(stage, slot)
        drain(stage)
        rest = [chunk for chunk in range(CHUNKS) if last[chunk] == SLOTS - 1]
        if stage == 0:
            late = [chunk for chunk in rest if chunk >= 2]
        for chunk in rest:
            if chunk not in late:
                pick(stage, chunk, source, goal)

    for chunk in range(CHUNKS):
        finish(chunk)
    for number in range(PARTS):
        store(number).wait()
    pltpu.make_async_copy(flat, flat_out, store_sem.at[PARTS]).wait()


def ring_move(plan, mine, left_table):
    width = mine.shape[-1]
    vmem = pl.BlockSpec(memory_space=pltpu.VMEM)
    smem = pl.BlockSpec(memory_space=pltpu.SMEM)
    hbm = pl.BlockSpec(memory_space=pl.ANY)
    bf16 = jnp.bfloat16
    return pl.pallas_call(
        ring_kernel,
        out_shape=[
            jax.ShapeDtypeStruct((TONES, SEGMENTS * 16, CHANNELS), bf16),
            jax.ShapeDtypeStruct((SEGMENTS * CHANNELS, 128), bf16),
            jax.ShapeDtypeStruct((ROWS, width), bf16),
            jax.ShapeDtypeStruct((ROWS, width), bf16),
        ],
        in_specs=[smem, smem, hbm, vmem],
        out_specs=[hbm, hbm, vmem, vmem],
        scratch_shapes=[
            pltpu.VMEM((2, ROWS, width), bf16),
            pltpu.VMEM((2, ROWS, width), bf16),
            pltpu.VMEM((ROWS, width), bf16),
            pltpu.VMEM((ROWS, width), bf16),
            pltpu.VMEM((ROWS, width), bf16),
            pltpu.VMEM((2, ROWS, width), bf16),
            pltpu.VMEM((2, ROWS, width), bf16),
            pltpu.VMEM((2, 4, STREAMS, SLOTS, PIECE, width), bf16),
            pltpu.VMEM((4, STREAMS, 2, PIECE, width), bf16),
            pltpu.VMEM((TONES * 16, 2 * BINS), bf16),
            pltpu.VMEM((2 * BINS, SEGMENTS * CHANNELS), bf16),
            pltpu.VMEM((TONES, SEGMENTS * 16, CHANNELS), bf16),
            pltpu.VMEM((SEGMENTS * CHANNELS, 128), bf16),
            pltpu.SemaphoreType.DMA((4, STREAMS, 2)),
            pltpu.SemaphoreType.DMA((2, 4, STREAMS, SLOTS)),
            pltpu.SemaphoreType.DMA((6, CHUNKS)),
            pltpu.SemaphoreType.DMA((6, CHUNKS)),
            pltpu.SemaphoreType.DMA,
            pltpu.SemaphoreType.DMA((PARTS + 1,)),
        ],
        compiler_params=pltpu.CompilerParams(
            collective_id=0, has_side_effects=True, vmem_limit_bytes=56 * 2**20
        ),
    )(plan, jnp.asarray(CODES), left_table, mine)


def window_tables():
    time = np.arange(1024)
    bins = np.arange(BINS)
    angle = 2 * np.pi * (np.outer(time, bins) % 1024) / 1024
    weight = np.where(bins == 0, np.sqrt(0.5), 1.0)
    samples = np.concatenate([np.cos(angle) * weight, -np.sin(angle) * weight], axis=1)
    tones = 2 * np.pi * (np.arange(TONES) + 0.5) / SPAN

    def table(offsets):
        turn = np.exp(-1j * np.outer(tones, offsets))
        result = np.empty((TONES, 2, WINDOWS, 2 * BINS))
        for window in range(WINDOWS):
            both = turn @ samples[(window * 128 + offsets) % 1024]
            result[:, 0, window], result[:, 1, window] = both.real, both.imag
        return (result / 32.0).reshape(TONES * 2 * WINDOWS, 2 * BINS)

    return table(np.arange(-64, 192)), table(np.arange(128))


def lag_tables():
    tones = 2 * np.pi * (np.arange(TONES // 2) + 0.5) / SPAN
    scale = 1024.0 / BINS * 2.0 / SPAN / math.sqrt(2.0 * SEGMENTS * BINS)
    even, late, odd = np.arange(0, 65, 2), np.arange(2, 65, 2), np.arange(1, 64, 2)
    parts = [np.cos(np.outer(even, tones)), np.sin(np.outer(late, tones))]
    parts += [np.cos(np.outer(odd, tones)), np.sin(np.outer(odd, tones))]
    return np.kron(np.concatenate(parts, axis=0) * scale, np.eye(8))


def correlate_kernel(right_table, lag_table, left_ref, flat_ref, near_ref, far_ref, out_ref,
                     right_rows, lag_rows, left_tones, flat, near, far, right_turned, right_tones, folded, constant, held,
                     load_sem, part_sem, out_sem):
    f32, bf16 = jnp.float32, jnp.bfloat16
    loads = [
        pltpu.make_async_copy(source, goal, load_sem.at[number])
        for number, (source, goal) in enumerate(
            [(near_ref, near), (far_ref, far), (flat_ref, flat), (left_ref, left_tones), (lag_table, lag_rows)]
        )
    ]

    def part_rows(number):
        return pl.ds(pl.multiple_of(number * STEP, STEP), STEP)

    def part_load(number):
        rows = part_rows(number)
        return pltpu.make_async_copy(right_table.at[rows, :], right_rows.at[rows, :], part_sem.at[number])

    def result(pair):
        rows = pl.ds(pl.multiple_of(pair * 16, 16), 16)
        return pltpu.make_async_copy(held.at[pair % 2], out_ref.at[:, rows, :], out_sem.at[pair % 2])

    for load in loads[:2]:
        load.start()
    for number in range(PARTS):
        part_load(number).start()
    for load in loads[2:]:
        load.start()

    loads[0].wait()
    lay_out(near, far, right_turned, range(3))
    loads[1].wait()
    lay_out(near, far, right_turned, range(3, 6))

    def tones_of(number, carry):
        part_load(number).wait()
        where = pl.ds(number * (STEP // 16), STEP // 16)
        right = jnp.dot(right_rows[part_rows(number), :], right_turned[...], preferred_element_type=f32)
        for segment in range(SEGMENTS):
            lanes = slice(segment * CHANNELS, (segment + 1) * CHANNELS)
            depth = slice(segment * 16, (segment + 1) * 16)
            plain = right[:, lanes].reshape(STEP // 16, 2, 8, CHANNELS)
            right_tones[where, depth, :CHANNELS] = plain.reshape(STEP // 16, 16, CHANNELS).astype(bf16)
            turned = jnp.concatenate([-plain[:, 1], plain[:, 0]], axis=1)
            right_tones[where, depth, CHANNELS:] = turned.astype(bf16)
        return carry

    lax.fori_loop(0, PARTS, tones_of, 0)

    loads[2].wait()
    total = jnp.zeros((CHANNELS, CHANNELS), f32)
    for segment in range(SEGMENTS):
        mine = flat[segment * CHANNELS:(segment + 1) * CHANNELS, :]
        theirs = sixth(near, far, segment, 1)[:, :128]
        total += lax.dot_general(mine, theirs, (((1,), (1,)), ((), ())), preferred_element_type=f32)
    constant[...] = total * (1.0 / math.sqrt(2.0 * SEGMENTS * BINS))
    loads[3].wait()

    def cross(tone):
        return jnp.dot(left_tones[tone].T, right_tones[tone], preferred_element_type=f32)

    def fold(number, carry):
        tone = number * 2
        pairs = []
        for offset in range(2):
            low, high = cross(tone + offset), cross(TONES - 1 - tone - offset)
            plus, minus = low + high, low - high
            pairs.append((plus[:, :128], minus[:, 128:], minus[:, :128], plus[:, 128:]))
        rows = pl.ds(pl.multiple_of(number * 16, 16), 16)
        for kind in range(4):
            one, two = pairs[0][kind], pairs[1][kind]
            for group in range(16):
                both = jnp.concatenate([one[group * 8:group * 8 + 8], two[group * 8:group * 8 + 8]], axis=0)
                lanes = slice((group % 2) * 128, (group % 2) * 128 + 128)
                folded[kind, group // 2, rows, lanes] = both.astype(bf16)
        return carry

    lax.fori_loop(0, TONES // 4, fold, 0, unroll=UNROLL)
    loads[4].wait()

    def lags(pair, carry):
        slot = pair % 2
        base = constant[pl.ds(pl.multiple_of(pair * 16, 16), 16), :]

        @pl.when(pair >= 2)
        def _():
            result(pair - 2).wait()

        def turn(kind, first, count):
            both = jnp.dot(lag_rows[first * 8:(first + count) * 8, :], folded[kind, pair], preferred_element_type=f32)
            both = both.reshape(count, 8, 256)
            return jnp.concatenate([both[:, :, :128], both[:, :, 128:]], axis=1)

        cosines, sines = turn(0, 0, 33) + base, turn(1, 33, 32)
        held[slot, 64, :, :] = cosines[0].astype(bf16)
        for lag in range(1, 33):
            if lag < 32:
                held[slot, 64 + 2 * lag, :, :] = (cosines[lag] - sines[lag - 1]).astype(bf16)
            held[slot, 64 - 2 * lag, :, :] = (cosines[lag] + sines[lag - 1]).astype(bf16)
        cosines, sines = turn(2, 65, 32) + base, turn(3, 97, 32)
        for lag in range(32):
            held[slot, 65 + 2 * lag, :, :] = (cosines[lag] - sines[lag]).astype(bf16)
            held[slot, 63 - 2 * lag, :, :] = (cosines[lag] + sines[lag]).astype(bf16)
        result(pair).start()
        return carry

    lax.fori_loop(0, CHANNELS // 16, lags, 0)
    result(CHANNELS // 16 - 2).wait()
    result(CHANNELS // 16 - 1).wait()


def correlate(left_tones, flat, near, far, right_table, lag_table):
    hbm = pl.BlockSpec(memory_space=pl.ANY)
    bf16 = jnp.bfloat16
    return pl.pallas_call(
        correlate_kernel,
        out_shape=jax.ShapeDtypeStruct((LAGS, CHANNELS, CHANNELS), bf16),
        in_specs=[hbm] * 6,
        out_specs=hbm,
        scratch_shapes=[
            pltpu.VMEM(right_table.shape, bf16),
            pltpu.VMEM(lag_table.shape, bf16),
            pltpu.VMEM(left_tones.shape, bf16),
            pltpu.VMEM(flat.shape, bf16),
            pltpu.VMEM(near.shape, bf16),
            pltpu.VMEM(far.shape, bf16),
            pltpu.VMEM((2 * BINS, SEGMENTS * CHANNELS), bf16),
            pltpu.VMEM((TONES, SEGMENTS * 16, 2 * CHANNELS), bf16),
            pltpu.VMEM((4, CHANNELS // 16, TONES // 2 * 8, 256), bf16),
            pltpu.VMEM((CHANNELS, CHANNELS), jnp.float32),
            pltpu.VMEM((2, LAGS, 16, CHANNELS), bf16),
            pltpu.SemaphoreType.DMA((5,)),
            pltpu.SemaphoreType.DMA((PARTS,)),
            pltpu.SemaphoreType.DMA((2,)),
        ],
        compiler_params=pltpu.CompilerParams(vmem_limit_bytes=56 * 2**20),
    )(right_table, lag_table, left_tones, flat, near, far)


def per_device(spectra, plan):
    left_table, right_table = (jnp.asarray(table, jnp.bfloat16) for table in window_tables())
    lag_table = jnp.asarray(lag_tables(), jnp.bfloat16)
    left_tones, flat, near, far = ring_move(plan, spectra.reshape(ROWS, BINS), left_table)
    return correlate(left_tones, flat, near, far, right_table, lag_table)[None, None]


def solution(mesh):
    in_specs = (P("ch", "seg", None, None, None), P(None, "ch"))
    out_specs = P("ch", "seg", None, None, None)
    return jax.shard_map(
        per_device, mesh=mesh, in_specs=in_specs, out_specs=out_specs, check_vma=False
    )
```

```python
import functools
import math

import jax
import jax.numpy as jnp
import numpy as np
from jax import lax
from jax.experimental import pallas as pl
from jax.experimental.pallas import tpu as pltpu
from jax.sharding import PartitionSpec as P

LAGS = 128
MESH = pl.DeviceIdType.MESH
RING = 8
CHUNKS = 4
SLOTS = 2 * CHUNKS
WIDTH = 2 * SLOTS + CHUNKS
STREAMS = 4
ROWS = 768
BLOCK = ROWS // CHUNKS
PIECE = BLOCK // STREAMS


def ring_plan():
    sends, lands = {}, {}

    def travel(mask, place, direction, chunk, slots):
        for hop, slot in enumerate(slots):
            at = (mask, (place + (hop if direction == 0 else -hop)) % RING, slot, direction)
            assert at not in sends and slot < SLOTS
            sends[at] = ("own", chunk) if hop == 0 else ("pass", slots[hop - 1])
        lands[mask, place ^ mask, chunk] = (direction, slots[-1])

    for mask in range(1, RING):
        for place in range(RING):
            ahead = ((place ^ mask) - place) % RING
            direction, hops = (0, ahead) if ahead <= 4 else (1, RING - ahead)
            for chunk in range(CHUNKS):
                if mask == 4:
                    travel(mask, place, chunk % 2, chunk, [4 * (chunk // 2) + hop for hop in range(4)])
                elif mask in (3, 7):
                    slots = [chunk, chunk + 1, chunk + 2] if hops == 3 else [CHUNKS + chunk if chunk else 0]
                    travel(mask, place, direction, chunk, slots)
                else:
                    slots = [[chunk], [chunk, CHUNKS + chunk], [chunk, chunk + 1, CHUNKS + chunk]][hops - 1]
                    travel(mask, place, direction, chunk, slots)

    sources = [
        [sorted({what for at, what in sends.items() if at[2:] == (slot, way)}) for way in range(2)] for slot in range(SLOTS)
    ]
    spots = [sorted({where for at, where in lands.items() if at[2] == chunk}) + [None] for chunk in range(CHUNKS)]
    table = np.zeros((RING, RING, WIDTH), np.int32)
    for (mask, place, slot, way), what in sends.items():
        table[mask, place, slot * 2 + way] = sources[slot][way].index(what)
    for chunk in range(CHUNKS):
        for mask in range(RING):
            for place in range(RING):
                table[mask, place, 2 * SLOTS + chunk] = spots[chunk].index(lands.get((mask, place, chunk)))
    return sources, spots, table.reshape(-1)


SOURCES, SPOTS, CODES = ring_plan()
BINS = 512
SEGMENTS = 6
CHANNELS = 128
WINDOWS = 8
TONES = 128
SPAN = 2 * TONES
STEP = 256
UNROLL = 8
PARTS = TONES * 16 // STEP


def sixth(near, far, segment, part):
    first = (segment % 3) * 2 * CHANNELS + part * CHANNELS
    return (near if segment < 3 else far)[first:first + CHANNELS, :]


def lay_out(near, far, turned, segments):
    for segment in segments:
        lanes = slice(segment * CHANNELS, (segment + 1) * CHANNELS)
        for part in range(2):
            turned[part * BINS:(part + 1) * BINS, lanes] = sixth(near, far, segment, part).T


def ring_kernel(plan_in, table_in, left_table, mine_in, tones_out, flat_out, near_out, far_out, first, middle, beside, across,
                opposite, chosen, swapped, landed, staged, left_rows, left_turned, left_tones, flat, send_sem, recv_sem, x_send,
                x_recv, load_sem, store_sem, plan_ref, table_ref, mine_ref):
    load = pltpu.make_async_copy(left_table, left_rows, load_sem.at[0])
    early = [
        pltpu.make_async_copy(source, goal, load_sem.at[number])
        for number, (source, goal) in enumerate([(mine_in, mine_ref), (plan_in, plan_ref), (table_in, table_ref)], 1)
    ]
    for copy in early:
        copy.start()
    ch, seg = lax.axis_index("ch"), lax.axis_index("seg")
    z, y = ch // 2 % RING, ch // 32
    turned = ch + 16 - ch // 16 % 2 * 32
    targets = [
        ((ch + 32) % 256, seg),
        ((ch + 224) % 256, seg),
        (ch - z * 2 + (z + 1) % RING * 2, seg),
        (ch - z * 2 + (z + RING - 1) % RING * 2, seg),
        (turned, seg),
        (turned, 1 - seg),
        (ch + 1 - ch % 2 * 2, seg),
    ]
    barrier = pltpu.get_barrier_semaphore()
    for target in targets:
        pl.semaphore_signal(barrier, inc=1, device_id=target, device_id_type=MESH)
    pl.semaphore_wait(barrier, len(targets))

    def rows(start, count):
        return pl.ds(pl.multiple_of(start, 16), count)

    def x_copy(kind, chunk):
        all_rows = rows(chunk * BLOCK, BLOCK)
        upper, lower = rows(chunk * BLOCK, BLOCK // 2), rows(chunk * BLOCK + BLOCK // 2, BLOCK // 2)
        source, goal, target = [
            (mine_in.at[all_rows, :], beside.at[all_rows, :], targets[4]),
            (mine_in.at[all_rows, :], across.at[all_rows, :], targets[5]),
            (beside.at[upper, :], opposite.at[upper, :], targets[5]),
            (across.at[lower, :], opposite.at[lower, :], targets[4]),
            (chosen.at[0, all_rows, :], swapped.at[0, all_rows, :], targets[6]),
            (chosen.at[1, all_rows, :], swapped.at[1, all_rows, :], targets[6]),
        ][kind]
        return pltpu.make_async_remote_copy(
            src_ref=source,
            dst_ref=goal,
            send_sem=x_send.at[kind, chunk],
            recv_sem=x_recv.at[kind, chunk],
            device_id=target,
            device_id_type=MESH,
        )

    def spread(chunk):
        for kind in (0, 1):
            x_copy(kind, chunk).start()

    def forward(chunk):
        for kind in (0, 1):
            x_copy(kind, chunk).wait_recv()
        for kind in (2, 3):
            x_copy(kind, chunk).start()

    def choose(chunk):
        for kind in (2, 3):
            x_copy(kind, chunk).wait_recv()
        here = rows(chunk * BLOCK, BLOCK)
        chosen[0, here, :] = jnp.where(x_bit == 1, beside[here, :], mine_ref[here, :])
        chosen[1, here, :] = jnp.where(x_bit == 1, across[here, :], opposite[here, :])
        for kind in (4, 5):
            x_copy(kind, chunk).start()

    def settle(chunk):
        here = rows(chunk * BLOCK, BLOCK)
        for half in range(2):
            x_copy(4 + half, chunk).wait_recv()
            first[half, here, :] = jnp.where(core_bit == 1, swapped[half, here, :], chosen[half, here, :])

    def finish(chunk):
        for kind in range(6):
            x_copy(kind, chunk).wait_send()

    def store(number):
        where = pl.ds(number * (STEP // 16), STEP // 16)
        return pltpu.make_async_copy(left_tones.at[where], tones_out.at[where], store_sem.at[number])

    def left_part(number):
        part = rows(number * STEP, STEP)
        tones = jnp.dot(left_rows[part, :], left_turned[...], preferred_element_type=jnp.float32)
        for segment in range(SEGMENTS):
            piece_tones = tones[:, segment * CHANNELS:(segment + 1) * CHANNELS].reshape(STEP // 16, 16, CHANNELS)
            depth = slice(segment * 16, (segment + 1) * 16)
            left_tones[pl.ds(number * (STEP // 16), STEP // 16), depth, :] = piece_tones.astype(jnp.bfloat16)
        store(number).start()

    def flatten():
        first_lane = lax.broadcasted_iota(jnp.int32, (CHANNELS, 128), 1) == 0
        for segment in range(SEGMENTS):
            value = sixth(mine_ref, opposite, segment, 1)[:, :128].astype(jnp.float32)
            flat[segment * CHANNELS:(segment + 1) * CHANNELS, :] = jnp.where(first_lane, value, 0.0).astype(jnp.bfloat16)
        pltpu.make_async_copy(flat, flat_out, store_sem.at[PARTS]).start()

    spread(0)
    spread(1)
    load.start()
    for copy in early:
        copy.wait()
    mask = plan_ref[seg, 0] ^ ch
    bases = [(((mask // 32) % RING) * RING + y) * WIDTH, (((mask // 2) % RING) * RING + z) * WIDTH]
    x_bit, core_bit = mask // 16 % 2, mask % 2
    forward(0)
    forward(1)
    choose(0)
    choose(1)
    spread(2)
    settle(0)
    settle(1)

    def beside_slot(stage, slot):
        if stage == 0:
            if slot == 0:
                forward(2)
                spread(3)
            elif slot == 1:
                choose(2)
                settle(2)
                forward(3)
            elif slot == 2:
                choose(3)
                settle(3)
            elif slot == 3:
                lay_out(mine_ref, opposite, left_turned, range(3))
            elif slot == 4:
                lay_out(mine_ref, opposite, left_turned, range(3, 6))
                flatten()
            elif slot == 5:
                load.wait()
            if slot >= 6:
                left_part(slot - 6)
        elif slot < 6:
            left_part(slot + 2)

    def ring_copy(stage, link, stream, slot):
        return pltpu.make_async_remote_copy(
            src_ref=staged.at[link, stream, slot % 2],
            dst_ref=landed.at[stage, link, stream, slot],
            send_sem=send_sem.at[link, stream, slot % 2],
            recv_sem=recv_sem.at[stage, link, stream, slot],
            device_id=targets[link],
            device_id_type=MESH,
        )

    def piece(stream, chunk):
        return rows(chunk * BLOCK + stream * PIECE, PIECE)

    def each_stream(body):
        def step(stream, carry):
            body(stream)
            return carry

        lax.fori_loop(0, STREAMS, step, 0)

    def send(stage, slot, source):
        def one(stream):
            for dim in range(2):
                for way in range(2):
                    link = 2 * dim + way
                    if slot >= 1:
                        ring_copy(stage, link, stream, slot - 1).wait_recv()
                    if slot >= 2:
                        ring_copy(stage, link, stream, slot - 2).wait_send()
                    code = table_ref[bases[dim] + slot * 2 + way]
                    value = None
                    for number, (kind, index) in enumerate(SOURCES[slot][way]):
                        if kind == "own":
                            option = source[dim ^ stage][piece(stream, index), :]
                        else:
                            option = landed[stage, link, stream, index]
                        value = option if value is None else jnp.where(code == number, option, value)
                    staged[link, stream, slot % 2] = value
                    ring_copy(stage, link, stream, slot).start()

        each_stream(one)

    def pick(stage, chunk, source, goal):
        def one(stream):
            for dim in range(2):
                code = table_ref[bases[dim] + 2 * SLOTS + chunk]
                value = source[dim ^ stage][piece(stream, chunk), :]
                for number, spot in enumerate(SPOTS[chunk][:-1]):
                    value = jnp.where(code == number, landed[stage, 2 * dim + spot[0], stream, spot[1]], value)
                goal[dim ^ stage][piece(stream, chunk), :] = value

        each_stream(one)

    def drain(stage):
        def one(stream):
            for link in range(4):
                ring_copy(stage, link, stream, SLOTS - 1).wait_recv()
                ring_copy(stage, link, stream, SLOTS - 2).wait_send()
                ring_copy(stage, link, stream, SLOTS - 1).wait_send()

        each_stream(one)

    last = [max(spot[1] for spot in spots[:-1]) for spots in SPOTS]
    sides = [(first.at[0], first.at[1]), (middle.at[0], middle.at[1]), (near_out, far_out)]
    late = []
    for stage in range(2):
        source, goal = sides[stage], sides[stage + 1]
        for slot in range(SLOTS):
            send(stage, slot, source)
            for chunk in late:
                pick(0, chunk, sides[0], sides[1])
            late = []
            for chunk in range(CHUNKS):
                if last[chunk] == slot - 1:
                    pick(stage, chunk, source, goal)
            beside_slot(stage, slot)
        drain(stage)
        rest = [chunk for chunk in range(CHUNKS) if last[chunk] == SLOTS - 1]
        if stage == 0:
            late = [chunk for chunk in rest if chunk >= 2]
        for chunk in rest:
            if chunk not in late:
                pick(stage, chunk, source, goal)

    for chunk in range(CHUNKS):
        finish(chunk)
    for number in range(PARTS):
        store(number).wait()
    pltpu.make_async_copy(flat, flat_out, store_sem.at[PARTS]).wait()


def ring_move(plan, mine, left_table):
    width = mine.shape[-1]
    vmem = pl.BlockSpec(memory_space=pltpu.VMEM)
    hbm = pl.BlockSpec(memory_space=pl.ANY)
    bf16 = jnp.bfloat16
    return pl.pallas_call(
        ring_kernel,
        out_shape=[
            jax.ShapeDtypeStruct((TONES, SEGMENTS * 16, CHANNELS), bf16),
            jax.ShapeDtypeStruct((SEGMENTS * CHANNELS, 128), bf16),
            jax.ShapeDtypeStruct((ROWS, width), bf16),
            jax.ShapeDtypeStruct((ROWS, width), bf16),
        ],
        in_specs=[hbm] * 4,
        out_specs=[hbm, hbm, vmem, vmem],
        scratch_shapes=[
            pltpu.VMEM((2, ROWS, width), bf16),
            pltpu.VMEM((2, ROWS, width), bf16),
            pltpu.VMEM((ROWS, width), bf16),
            pltpu.VMEM((ROWS, width), bf16),
            pltpu.VMEM((ROWS, width), bf16),
            pltpu.VMEM((2, ROWS, width), bf16),
            pltpu.VMEM((2, ROWS, width), bf16),
            pltpu.VMEM((2, 4, STREAMS, SLOTS, PIECE, width), bf16),
            pltpu.VMEM((4, STREAMS, 2, PIECE, width), bf16),
            pltpu.VMEM((TONES * 16, 2 * BINS), bf16),
            pltpu.VMEM((2 * BINS, SEGMENTS * CHANNELS), bf16),
            pltpu.VMEM((TONES, SEGMENTS * 16, CHANNELS), bf16),
            pltpu.VMEM((SEGMENTS * CHANNELS, 128), bf16),
            pltpu.SemaphoreType.DMA((4, STREAMS, 2)),
            pltpu.SemaphoreType.DMA((2, 4, STREAMS, SLOTS)),
            pltpu.SemaphoreType.DMA((6, CHUNKS)),
            pltpu.SemaphoreType.DMA((6, CHUNKS)),
            pltpu.SemaphoreType.DMA((4,)),
            pltpu.SemaphoreType.DMA((PARTS + 1,)),
            pltpu.SMEM(plan.shape, jnp.int32),
            pltpu.SMEM(CODES.shape, jnp.int32),
            pltpu.VMEM((ROWS, width), bf16),
        ],
        compiler_params=pltpu.CompilerParams(
            collective_id=0, has_side_effects=True, vmem_limit_bytes=56 * 2**20
        ),
    )(plan, jnp.asarray(CODES), left_table, mine)


def window_tables():
    time = np.arange(1024)
    bins = np.arange(BINS)
    angle = 2 * np.pi * (np.outer(time, bins) % 1024) / 1024
    weight = np.where(bins == 0, np.sqrt(0.5), 1.0)
    samples = np.concatenate([np.cos(angle) * weight, -np.sin(angle) * weight], axis=1)
    tones = 2 * np.pi * (np.arange(TONES) + 0.5) / SPAN

    def table(offsets):
        turn = np.exp(-1j * np.outer(tones, offsets))
        result = np.empty((TONES, 2, WINDOWS, 2 * BINS))
        for window in range(WINDOWS):
            both = turn @ samples[(window * 128 + offsets) % 1024]
            result[:, 0, window], result[:, 1, window] = both.real, both.imag
        return (result / 32.0).reshape(TONES * 2 * WINDOWS, 2 * BINS)

    return table(np.arange(-64, 192)), table(np.arange(128))


def lag_tables():
    tones = 2 * np.pi * (np.arange(TONES // 2) + 0.5) / SPAN
    scale = 1024.0 / BINS * 2.0 / SPAN / math.sqrt(2.0 * SEGMENTS * BINS)
    even, late, odd = np.arange(0, 65, 2), np.arange(2, 65, 2), np.arange(1, 64, 2)
    parts = [np.cos(np.outer(even, tones)), np.sin(np.outer(late, tones))]
    parts += [np.cos(np.outer(odd, tones)), np.sin(np.outer(odd, tones))]
    return np.kron(np.concatenate(parts, axis=0) * scale, np.eye(8))


def correlate_kernel(right_table, lag_table, left_ref, flat_ref, near_ref, far_ref, out_ref,
                     right_rows, lag_rows, left_tones, flat, near, far, right_turned, right_tones, folded, constant, held,
                     load_sem, part_sem, out_sem):
    f32, bf16 = jnp.float32, jnp.bfloat16
    loads = [
        pltpu.make_async_copy(source, goal, load_sem.at[number])
        for number, (source, goal) in enumerate(
            [(near_ref, near), (far_ref, far), (flat_ref, flat), (left_ref, left_tones), (lag_table, lag_rows)]
        )
    ]

    def part_rows(number):
        return pl.ds(pl.multiple_of(number * STEP, STEP), STEP)

    def part_load(number):
        rows = part_rows(number)
        return pltpu.make_async_copy(right_table.at[rows, :], right_rows.at[rows, :], part_sem.at[number])

    def result(pair):
        rows = pl.ds(pl.multiple_of(pair * 16, 16), 16)
        return pltpu.make_async_copy(held.at[pair % 2], out_ref.at[:, rows, :], out_sem.at[pair % 2])

    for load in loads[:2]:
        load.start()
    for number in range(PARTS):
        part_load(number).start()
    for load in loads[2:]:
        load.start()

    loads[0].wait()
    lay_out(near, far, right_turned, range(3))
    loads[1].wait()
    lay_out(near, far, right_turned, range(3, 6))

    def tones_of(number, carry):
        part_load(number).wait()
        where = pl.ds(number * (STEP // 16), STEP // 16)
        right = jnp.dot(right_rows[part_rows(number), :], right_turned[...], preferred_element_type=f32)
        for segment in range(SEGMENTS):
            lanes = slice(segment * CHANNELS, (segment + 1) * CHANNELS)
            depth = slice(segment * 16, (segment + 1) * 16)
            plain = right[:, lanes].reshape(STEP // 16, 2, 8, CHANNELS)
            right_tones[where, depth, :CHANNELS] = plain.reshape(STEP // 16, 16, CHANNELS).astype(bf16)
            turned = jnp.concatenate([-plain[:, 1], plain[:, 0]], axis=1)
            right_tones[where, depth, CHANNELS:] = turned.astype(bf16)
        return carry

    lax.fori_loop(0, PARTS, tones_of, 0)

    loads[2].wait()
    total = jnp.zeros((CHANNELS, CHANNELS), f32)
    for segment in range(SEGMENTS):
        mine = flat[segment * CHANNELS:(segment + 1) * CHANNELS, :]
        theirs = sixth(near, far, segment, 1)[:, :128]
        total += lax.dot_general(mine, theirs, (((1,), (1,)), ((), ())), preferred_element_type=f32)
    constant[...] = total * (1.0 / math.sqrt(2.0 * SEGMENTS * BINS))
    loads[3].wait()

    def cross(tone):
        return jnp.dot(left_tones[tone].T, right_tones[tone], preferred_element_type=f32)

    def fold(number, carry):
        tone = number * 2
        pairs = []
        for offset in range(2):
            low, high = cross(tone + offset), cross(TONES - 1 - tone - offset)
            plus, minus = low + high, low - high
            pairs.append((plus[:, :128], minus[:, 128:], minus[:, :128], plus[:, 128:]))
        rows = pl.ds(pl.multiple_of(number * 16, 16), 16)
        for kind in range(4):
            one, two = pairs[0][kind], pairs[1][kind]
            for group in range(16):
                both = jnp.concatenate([one[group * 8:group * 8 + 8], two[group * 8:group * 8 + 8]], axis=0)
                lanes = slice((group % 2) * 128, (group % 2) * 128 + 128)
                folded[kind, group // 2, rows, lanes] = both.astype(bf16)
        return carry

    lax.fori_loop(0, TONES // 4, fold, 0, unroll=UNROLL)
    loads[4].wait()

    def lags(pair, carry):
        slot = pair % 2
        base = constant[pl.ds(pl.multiple_of(pair * 16, 16), 16), :]

        @pl.when(pair >= 2)
        def _():
            result(pair - 2).wait()

        def turn(kind, first, count):
            both = jnp.dot(lag_rows[first * 8:(first + count) * 8, :], folded[kind, pair], preferred_element_type=f32)
            both = both.reshape(count, 8, 256)
            return jnp.concatenate([both[:, :, :128], both[:, :, 128:]], axis=1)

        cosines, sines = turn(0, 0, 33) + base, turn(1, 33, 32)
        held[slot, 64, :, :] = cosines[0].astype(bf16)
        for lag in range(1, 33):
            if lag < 32:
                held[slot, 64 + 2 * lag, :, :] = (cosines[lag] - sines[lag - 1]).astype(bf16)
            held[slot, 64 - 2 * lag, :, :] = (cosines[lag] + sines[lag - 1]).astype(bf16)
        cosines, sines = turn(2, 65, 32) + base, turn(3, 97, 32)
        for lag in range(32):
            held[slot, 65 + 2 * lag, :, :] = (cosines[lag] - sines[lag]).astype(bf16)
            held[slot, 63 - 2 * lag, :, :] = (cosines[lag] + sines[lag]).astype(bf16)
        result(pair).start()
        return carry

    lax.fori_loop(0, CHANNELS // 16, lags, 0)
    result(CHANNELS // 16 - 2).wait()
    result(CHANNELS // 16 - 1).wait()


def correlate(left_tones, flat, near, far, right_table, lag_table):
    hbm = pl.BlockSpec(memory_space=pl.ANY)
    bf16 = jnp.bfloat16
    return pl.pallas_call(
        correlate_kernel,
        out_shape=jax.ShapeDtypeStruct((LAGS, CHANNELS, CHANNELS), bf16),
        in_specs=[hbm] * 6,
        out_specs=hbm,
        scratch_shapes=[
            pltpu.VMEM(right_table.shape, bf16),
            pltpu.VMEM(lag_table.shape, bf16),
            pltpu.VMEM(left_tones.shape, bf16),
            pltpu.VMEM(flat.shape, bf16),
            pltpu.VMEM(near.shape, bf16),
            pltpu.VMEM(far.shape, bf16),
            pltpu.VMEM((2 * BINS, SEGMENTS * CHANNELS), bf16),
            pltpu.VMEM((TONES, SEGMENTS * 16, 2 * CHANNELS), bf16),
            pltpu.VMEM((4, CHANNELS // 16, TONES // 2 * 8, 256), bf16),
            pltpu.VMEM((CHANNELS, CHANNELS), jnp.float32),
            pltpu.VMEM((2, LAGS, 16, CHANNELS), bf16),
            pltpu.SemaphoreType.DMA((5,)),
            pltpu.SemaphoreType.DMA((PARTS,)),
            pltpu.SemaphoreType.DMA((2,)),
        ],
        compiler_params=pltpu.CompilerParams(vmem_limit_bytes=56 * 2**20),
    )(right_table, lag_table, left_tones, flat, near, far)


def per_device(spectra, plan):
    left_table, right_table = (jnp.asarray(table, jnp.bfloat16) for table in window_tables())
    lag_table = jnp.asarray(lag_tables(), jnp.bfloat16)
    left_tones, flat, near, far = ring_move(plan, spectra.reshape(ROWS, BINS), left_table)
    return correlate(left_tones, flat, near, far, right_table, lag_table)[None, None]


def solution(mesh):
    in_specs = (P("ch", "seg", None, None, None), P(None, "ch"))
    out_specs = P("ch", "seg", None, None, None)
    return jax.shard_map(
        per_device, mesh=mesh, in_specs=in_specs, out_specs=out_specs, check_vma=False
    )
```

```python
import functools
import math

import jax
import jax.numpy as jnp
import numpy as np
from jax import lax
from jax.experimental import pallas as pl
from jax.experimental.pallas import tpu as pltpu
from jax.sharding import PartitionSpec as P

LAGS = 128
MESH = pl.DeviceIdType.MESH
RING = 8
CHUNKS = 4
SLOTS = 2 * CHUNKS
WIDTH = 2 * SLOTS + CHUNKS
STREAMS = 4
ROWS = 768
BLOCK = ROWS // CHUNKS
PIECE = BLOCK // STREAMS


def ring_plan():
    sends, lands = {}, {}

    def travel(mask, place, direction, chunk, slots):
        for hop, slot in enumerate(slots):
            at = (mask, (place + (hop if direction == 0 else -hop)) % RING, slot, direction)
            assert at not in sends and slot < SLOTS
            sends[at] = ("own", chunk) if hop == 0 else ("pass", slots[hop - 1])
        lands[mask, place ^ mask, chunk] = (direction, slots[-1])

    for mask in range(1, RING):
        for place in range(RING):
            ahead = ((place ^ mask) - place) % RING
            direction, hops = (0, ahead) if ahead <= 4 else (1, RING - ahead)
            for chunk in range(CHUNKS):
                go, rest = (0, 1, 3, 5)[chunk], (2, 4, 6, 7)[chunk]
                if mask == 4:
                    travel(mask, place, chunk % 2, chunk, [4 * (chunk // 2) + hop for hop in range(4)])
                elif mask in (3, 7):
                    travel(mask, place, direction, chunk, [go, go + 1, go + 2] if hops == 3 else [(0, 3, 5, 7)[chunk]])
                else:
                    travel(mask, place, direction, chunk, [[go], [go, rest], [go, go + 1, rest]][hops - 1])

    sources = [
        [sorted({what for at, what in sends.items() if at[2:] == (slot, way)}) for way in range(2)] for slot in range(SLOTS)
    ]
    spots = [sorted({where for at, where in lands.items() if at[2] == chunk}) + [None] for chunk in range(CHUNKS)]
    table = np.zeros((RING, RING, WIDTH), np.int32)
    for (mask, place, slot, way), what in sends.items():
        table[mask, place, slot * 2 + way] = sources[slot][way].index(what)
    for chunk in range(CHUNKS):
        for mask in range(RING):
            for place in range(RING):
                table[mask, place, 2 * SLOTS + chunk] = spots[chunk].index(lands.get((mask, place, chunk)))
    return sources, spots, table.reshape(-1)


SOURCES, SPOTS, CODES = ring_plan()
BINS = 512
SEGMENTS = 6
CHANNELS = 128
WINDOWS = 8
TONES = 128
SPAN = 2 * TONES
STEP = 256
UNROLL = 8
PARTS = TONES * 16 // STEP


def sixth(near, far, segment, part):
    first = (segment % 3) * 2 * CHANNELS + part * CHANNELS
    return (near if segment < 3 else far)[first:first + CHANNELS, :]


def lay_out(near, far, turned, segments):
    for segment in segments:
        lanes = slice(segment * CHANNELS, (segment + 1) * CHANNELS)
        for part in range(2):
            turned[part * BINS:(part + 1) * BINS, lanes] = sixth(near, far, segment, part).T


def ring_kernel(plan_in, table_in, left_table, mine_in, tones_out, flat_out, near_out, far_out, first, middle, beside, across,
                opposite, chosen, swapped, landed, staged, left_rows, left_turned, left_tones, flat, send_sem, recv_sem, x_send,
                x_recv, load_sem, store_sem, plan_ref, table_ref, mine_ref):
    load = pltpu.make_async_copy(left_table, left_rows, load_sem.at[0])
    early = [
        pltpu.make_async_copy(source, goal, load_sem.at[number])
        for number, (source, goal) in enumerate([(mine_in, mine_ref), (plan_in, plan_ref), (table_in, table_ref)], 1)
    ]
    for copy in early:
        copy.start()
    ch, seg = lax.axis_index("ch"), lax.axis_index("seg")
    z, y = ch // 2 % RING, ch // 32
    turned = ch + 16 - ch // 16 % 2 * 32
    targets = [
        ((ch + 32) % 256, seg),
        ((ch + 224) % 256, seg),
        (ch - z * 2 + (z + 1) % RING * 2, seg),
        (ch - z * 2 + (z + RING - 1) % RING * 2, seg),
        (turned, seg),
        (turned, 1 - seg),
        (ch + 1 - ch % 2 * 2, seg),
    ]
    barrier = pltpu.get_barrier_semaphore()
    for target in targets:
        pl.semaphore_signal(barrier, inc=1, device_id=target, device_id_type=MESH)
    pl.semaphore_wait(barrier, len(targets))

    def rows(start, count):
        return pl.ds(pl.multiple_of(start, 16), count)

    def x_copy(kind, chunk):
        all_rows = rows(chunk * BLOCK, BLOCK)
        upper, lower = rows(chunk * BLOCK, BLOCK // 2), rows(chunk * BLOCK + BLOCK // 2, BLOCK // 2)
        source, goal, target = [
            (mine_in.at[all_rows, :], beside.at[all_rows, :], targets[4]),
            (mine_in.at[all_rows, :], across.at[all_rows, :], targets[5]),
            (beside.at[upper, :], opposite.at[upper, :], targets[5]),
            (across.at[lower, :], opposite.at[lower, :], targets[4]),
            (chosen.at[0, all_rows, :], swapped.at[0, all_rows, :], targets[6]),
            (chosen.at[1, all_rows, :], swapped.at[1, all_rows, :], targets[6]),
        ][kind]
        return pltpu.make_async_remote_copy(
            src_ref=source,
            dst_ref=goal,
            send_sem=x_send.at[kind, chunk],
            recv_sem=x_recv.at[kind, chunk],
            device_id=target,
            device_id_type=MESH,
        )

    def spread(chunk):
        for kind in (0, 1):
            x_copy(kind, chunk).start()

    def forward(chunk):
        for kind in (0, 1):
            x_copy(kind, chunk).wait_recv()
        for kind in (2, 3):
            x_copy(kind, chunk).start()

    def choose(chunk):
        for kind in (2, 3):
            x_copy(kind, chunk).wait_recv()
        here = rows(chunk * BLOCK, BLOCK)
        chosen[0, here, :] = jnp.where(x_bit == 1, beside[here, :], mine_ref[here, :])
        chosen[1, here, :] = jnp.where(x_bit == 1, across[here, :], opposite[here, :])
        for kind in (4, 5):
            x_copy(kind, chunk).start()

    def settle(chunk):
        here = rows(chunk * BLOCK, BLOCK)
        for half in range(2):
            x_copy(4 + half, chunk).wait_recv()
            first[half, here, :] = jnp.where(core_bit == 1, swapped[half, here, :], chosen[half, here, :])

    def finish(chunk):
        for kind in range(6):
            x_copy(kind, chunk).wait_send()

    def store(number):
        where = pl.ds(number * (STEP // 16), STEP // 16)
        return pltpu.make_async_copy(left_tones.at[where], tones_out.at[where], store_sem.at[number])

    def left_part(number):
        part = rows(number * STEP, STEP)
        tones = jnp.dot(left_rows[part, :], left_turned[...], preferred_element_type=jnp.float32)
        for segment in range(SEGMENTS):
            piece_tones = tones[:, segment * CHANNELS:(segment + 1) * CHANNELS].reshape(STEP // 16, 16, CHANNELS)
            depth = slice(segment * 16, (segment + 1) * 16)
            left_tones[pl.ds(number * (STEP // 16), STEP // 16), depth, :] = piece_tones.astype(jnp.bfloat16)
        store(number).start()

    def flatten():
        first_lane = lax.broadcasted_iota(jnp.int32, (CHANNELS, 128), 1) == 0
        for segment in range(SEGMENTS):
            value = sixth(mine_ref, opposite, segment, 1)[:, :128].astype(jnp.float32)
            flat[segment * CHANNELS:(segment + 1) * CHANNELS, :] = jnp.where(first_lane, value, 0.0).astype(jnp.bfloat16)
        pltpu.make_async_copy(flat, flat_out, store_sem.at[PARTS]).start()

    spread(0)
    spread(1)
    load.start()
    for copy in early:
        copy.wait()
    mask = plan_ref[0, seg] ^ ch
    bases = [(((mask // 32) % RING) * RING + y) * WIDTH, (((mask // 2) % RING) * RING + z) * WIDTH]
    x_bit, core_bit = mask // 16 % 2, mask % 2
    forward(0)
    forward(1)
    choose(0)
    choose(1)
    spread(2)
    settle(0)
    settle(1)

    def beside_slot(stage, slot):
        if stage == 0:
            if slot == 0:
                forward(2)
                spread(3)
            elif slot == 1:
                choose(2)
                forward(3)
            elif slot == 2:
                settle(2)
                choose(3)
            elif slot == 3:
                settle(3)
                lay_out(mine_ref, opposite, left_turned, range(3))
            elif slot == 4:
                lay_out(mine_ref, opposite, left_turned, range(3, 6))
                flatten()
            elif slot == 5:
                load.wait()
            if slot >= 6:
                left_part(slot - 6)
        elif slot < 6:
            left_part(slot + 2)

    def ring_copy(stage, link, stream, slot):
        return pltpu.make_async_remote_copy(
            src_ref=staged.at[link, stream, slot % 2],
            dst_ref=landed.at[stage, link, stream, slot],
            send_sem=send_sem.at[link, stream, slot % 2],
            recv_sem=recv_sem.at[stage, link, stream, slot],
            device_id=targets[link],
            device_id_type=MESH,
        )

    def piece(stream, chunk):
        return rows(chunk * BLOCK + stream * PIECE, PIECE)

    def each_stream(body):
        def step(stream, carry):
            body(stream)
            return carry

        lax.fori_loop(0, STREAMS, step, 0)

    def send(stage, slot, source):
        def one(stream):
            for dim in range(2):
                for way in range(2):
                    link = 2 * dim + way
                    if slot >= 1:
                        ring_copy(stage, link, stream, slot - 1).wait_recv()
                    if slot >= 2:
                        ring_copy(stage, link, stream, slot - 2).wait_send()
                    code = table_ref[bases[dim] + slot * 2 + way]
                    value = None
                    for number, (kind, index) in enumerate(SOURCES[slot][way]):
                        if kind == "own":
                            option = source[dim ^ stage][piece(stream, index), :]
                        else:
                            option = landed[stage, link, stream, index]
                        value = option if value is None else jnp.where(code == number, option, value)
                    staged[link, stream, slot % 2] = value
                    ring_copy(stage, link, stream, slot).start()

        each_stream(one)

    def pick(stage, chunk, source, goal):
        def one(stream):
            for dim in range(2):
                code = table_ref[bases[dim] + 2 * SLOTS + chunk]
                value = source[dim ^ stage][piece(stream, chunk), :]
                for number, spot in enumerate(SPOTS[chunk][:-1]):
                    value = jnp.where(code == number, landed[stage, 2 * dim + spot[0], stream, spot[1]], value)
                goal[dim ^ stage][piece(stream, chunk), :] = value

        each_stream(one)

    def drain(stage):
        def one(stream):
            for link in range(4):
                ring_copy(stage, link, stream, SLOTS - 1).wait_recv()
                ring_copy(stage, link, stream, SLOTS - 2).wait_send()
                ring_copy(stage, link, stream, SLOTS - 1).wait_send()

        each_stream(one)

    last = [max(spot[1] for spot in spots[:-1]) for spots in SPOTS]
    sides = [(first.at[0], first.at[1]), (middle.at[0], middle.at[1]), (near_out, far_out)]
    late = []
    for stage in range(2):
        source, goal = sides[stage], sides[stage + 1]
        for slot in range(SLOTS):
            send(stage, slot, source)
            for chunk in late:
                pick(0, chunk, sides[0], sides[1])
            late = []
            for chunk in range(CHUNKS):
                if last[chunk] == slot - 1:
                    pick(stage, chunk, source, goal)
            beside_slot(stage, slot)
        drain(stage)
        rest = [chunk for chunk in range(CHUNKS) if last[chunk] == SLOTS - 1]
        if stage == 0:
            late = [chunk for chunk in rest if chunk >= 2]
        for chunk in rest:
            if chunk not in late:
                pick(stage, chunk, source, goal)

    for chunk in range(CHUNKS):
        finish(chunk)
    for number in range(PARTS):
        store(number).wait()
    pltpu.make_async_copy(flat, flat_out, store_sem.at[PARTS]).wait()


def ring_move(plan, mine, left_table):
    width = mine.shape[-1]
    vmem = pl.BlockSpec(memory_space=pltpu.VMEM)
    hbm = pl.BlockSpec(memory_space=pl.ANY)
    bf16 = jnp.bfloat16
    return pl.pallas_call(
        ring_kernel,
        out_shape=[
            jax.ShapeDtypeStruct((TONES, SEGMENTS * 16, CHANNELS), bf16),
            jax.ShapeDtypeStruct((SEGMENTS * CHANNELS, 128), bf16),
            jax.ShapeDtypeStruct((ROWS, width), bf16),
            jax.ShapeDtypeStruct((ROWS, width), bf16),
        ],
        in_specs=[hbm] * 4,
        out_specs=[hbm, hbm, vmem, vmem],
        scratch_shapes=[
            pltpu.VMEM((2, ROWS, width), bf16),
            pltpu.VMEM((2, ROWS, width), bf16),
            pltpu.VMEM((ROWS, width), bf16),
            pltpu.VMEM((ROWS, width), bf16),
            pltpu.VMEM((ROWS, width), bf16),
            pltpu.VMEM((2, ROWS, width), bf16),
            pltpu.VMEM((2, ROWS, width), bf16),
            pltpu.VMEM((2, 4, STREAMS, SLOTS, PIECE, width), bf16),
            pltpu.VMEM((4, STREAMS, 2, PIECE, width), bf16),
            pltpu.VMEM((TONES * 16, 2 * BINS), bf16),
            pltpu.VMEM((2 * BINS, SEGMENTS * CHANNELS), bf16),
            pltpu.VMEM((TONES, SEGMENTS * 16, CHANNELS), bf16),
            pltpu.VMEM((SEGMENTS * CHANNELS, 128), bf16),
            pltpu.SemaphoreType.DMA((4, STREAMS, 2)),
            pltpu.SemaphoreType.DMA((2, 4, STREAMS, SLOTS)),
            pltpu.SemaphoreType.DMA((6, CHUNKS)),
            pltpu.SemaphoreType.DMA((6, CHUNKS)),
            pltpu.SemaphoreType.DMA((4,)),
            pltpu.SemaphoreType.DMA((PARTS + 1,)),
            pltpu.SMEM((1, plan.shape[0]), jnp.int32),
            pltpu.SMEM(CODES.shape, jnp.int32),
            pltpu.VMEM((ROWS, width), bf16),
        ],
        compiler_params=pltpu.CompilerParams(
            collective_id=0, has_side_effects=True, vmem_limit_bytes=56 * 2**20
        ),
    )(plan.T, jnp.asarray(CODES), left_table, mine)


def window_tables():
    time = np.arange(1024)
    bins = np.arange(BINS)
    angle = 2 * np.pi * (np.outer(time, bins) % 1024) / 1024
    weight = np.where(bins == 0, np.sqrt(0.5), 1.0)
    samples = np.concatenate([np.cos(angle) * weight, -np.sin(angle) * weight], axis=1)
    tones = 2 * np.pi * (np.arange(TONES) + 0.5) / SPAN

    def table(offsets):
        turn = np.exp(-1j * np.outer(tones, offsets))
        result = np.empty((TONES, 2, WINDOWS, 2 * BINS))
        for window in range(WINDOWS):
            both = turn @ samples[(window * 128 + offsets) % 1024]
            result[:, 0, window], result[:, 1, window] = both.real, both.imag
        return (result / 32.0).reshape(TONES * 2 * WINDOWS, 2 * BINS)

    return table(np.arange(-64, 192)), table(np.arange(128))


def lag_tables():
    tones = 2 * np.pi * (np.arange(TONES // 2) + 0.5) / SPAN
    scale = 1024.0 / BINS * 2.0 / SPAN / math.sqrt(2.0 * SEGMENTS * BINS)
    even, late, odd = np.arange(0, 65, 2), np.arange(2, 65, 2), np.arange(1, 64, 2)
    parts = [np.cos(np.outer(even, tones)), np.sin(np.outer(late, tones))]
    parts += [np.cos(np.outer(odd, tones)), np.sin(np.outer(odd, tones))]
    return np.kron(np.concatenate(parts, axis=0) * scale, np.eye(8))


def correlate_kernel(right_table, lag_table, left_ref, flat_ref, near_ref, far_ref, out_ref,
                     right_rows, lag_rows, left_tones, flat, near, far, right_turned, right_tones, folded, constant, held,
                     load_sem, part_sem, out_sem):
    f32, bf16 = jnp.float32, jnp.bfloat16
    loads = [
        pltpu.make_async_copy(source, goal, load_sem.at[number])
        for number, (source, goal) in enumerate(
            [(near_ref, near), (far_ref, far), (flat_ref, flat), (left_ref, left_tones), (lag_table, lag_rows)]
        )
    ]

    def part_rows(number):
        return pl.ds(pl.multiple_of(number * STEP, STEP), STEP)

    def part_load(number):
        rows = part_rows(number)
        return pltpu.make_async_copy(right_table.at[rows, :], right_rows.at[rows, :], part_sem.at[number])

    def result(pair):
        rows = pl.ds(pl.multiple_of(pair * 16, 16), 16)
        return pltpu.make_async_copy(held.at[pair % 2], out_ref.at[:, rows, :], out_sem.at[pair % 2])

    for load in loads[:2]:
        load.start()
    for number in range(2):
        part_load(number).start()

    loads[0].wait()
    lay_out(near, far, right_turned, range(3))
    loads[1].wait()
    for number in range(2, PARTS):
        part_load(number).start()
    for load in loads[2:]:
        load.start()
    lay_out(near, far, right_turned, range(3, 6))

    def tones_of(number, carry):
        part_load(number).wait()
        where = pl.ds(number * (STEP // 16), STEP // 16)
        right = jnp.dot(right_rows[part_rows(number), :], right_turned[...], preferred_element_type=f32)
        for segment in range(SEGMENTS):
            lanes = slice(segment * CHANNELS, (segment + 1) * CHANNELS)
            depth = slice(segment * 16, (segment + 1) * 16)
            plain = right[:, lanes].reshape(STEP // 16, 2, 8, CHANNELS)
            right_tones[where, depth, :CHANNELS] = plain.reshape(STEP // 16, 16, CHANNELS).astype(bf16)
            turned = jnp.concatenate([-plain[:, 1], plain[:, 0]], axis=1)
            right_tones[where, depth, CHANNELS:] = turned.astype(bf16)
        return carry

    lax.fori_loop(0, PARTS, tones_of, 0)

    loads[2].wait()
    total = jnp.zeros((CHANNELS, CHANNELS), f32)
    for segment in range(SEGMENTS):
        mine = flat[segment * CHANNELS:(segment + 1) * CHANNELS, :]
        theirs = sixth(near, far, segment, 1)[:, :128]
        total += lax.dot_general(mine, theirs, (((1,), (1,)), ((), ())), preferred_element_type=f32)
    constant[...] = total * (1.0 / math.sqrt(2.0 * SEGMENTS * BINS))
    loads[3].wait()

    def cross(tone):
        return jnp.dot(left_tones[tone].T, right_tones[tone], preferred_element_type=f32)

    def fold(number, carry):
        tone = number * 2
        pairs = []
        for offset in range(2):
            low, high = cross(tone + offset), cross(TONES - 1 - tone - offset)
            plus, minus = low + high, low - high
            pairs.append((plus[:, :128], minus[:, 128:], minus[:, :128], plus[:, 128:]))
        rows = pl.ds(pl.multiple_of(number * 16, 16), 16)
        for kind in range(4):
            one, two = pairs[0][kind], pairs[1][kind]
            for group in range(16):
                both = jnp.concatenate([one[group * 8:group * 8 + 8], two[group * 8:group * 8 + 8]], axis=0)
                lanes = slice((group % 2) * 128, (group % 2) * 128 + 128)
                folded[kind, group // 2, rows, lanes] = both.astype(bf16)
        return carry

    lax.fori_loop(0, TONES // 4, fold, 0, unroll=UNROLL)
    loads[4].wait()

    def lags(pair, carry):
        slot = pair % 2
        base = constant[pl.ds(pl.multiple_of(pair * 16, 16), 16), :]

        @pl.when(pair >= 2)
        def _():
            result(pair - 2).wait()

        def turn(kind, first, count):
            both = jnp.dot(lag_rows[first * 8:(first + count) * 8, :], folded[kind, pair], preferred_element_type=f32)
            both = both.reshape(count, 8, 256)
            return jnp.concatenate([both[:, :, :128], both[:, :, 128:]], axis=1)

        cosines, sines = turn(0, 0, 33) + base, turn(1, 33, 32)
        held[slot, 64, :, :] = cosines[0].astype(bf16)
        for lag in range(1, 33):
            if lag < 32:
                held[slot, 64 + 2 * lag, :, :] = (cosines[lag] - sines[lag - 1]).astype(bf16)
            held[slot, 64 - 2 * lag, :, :] = (cosines[lag] + sines[lag - 1]).astype(bf16)
        cosines, sines = turn(2, 65, 32) + base, turn(3, 97, 32)
        for lag in range(32):
            held[slot, 65 + 2 * lag, :, :] = (cosines[lag] - sines[lag]).astype(bf16)
            held[slot, 63 - 2 * lag, :, :] = (cosines[lag] + sines[lag]).astype(bf16)
        result(pair).start()
        return carry

    lax.fori_loop(0, CHANNELS // 16, lags, 0)
    result(CHANNELS // 16 - 2).wait()
    result(CHANNELS // 16 - 1).wait()


def correlate(left_tones, flat, near, far, right_table, lag_table):
    hbm = pl.BlockSpec(memory_space=pl.ANY)
    bf16 = jnp.bfloat16
    return pl.pallas_call(
        correlate_kernel,
        out_shape=jax.ShapeDtypeStruct((LAGS, CHANNELS, CHANNELS), bf16),
        in_specs=[hbm] * 6,
        out_specs=hbm,
        scratch_shapes=[
            pltpu.VMEM(right_table.shape, bf16),
            pltpu.VMEM(lag_table.shape, bf16),
            pltpu.VMEM(left_tones.shape, bf16),
            pltpu.VMEM(flat.shape, bf16),
            pltpu.VMEM(near.shape, bf16),
            pltpu.VMEM(far.shape, bf16),
            pltpu.VMEM((2 * BINS, SEGMENTS * CHANNELS), bf16),
            pltpu.VMEM((TONES, SEGMENTS * 16, 2 * CHANNELS), bf16),
            pltpu.VMEM((4, CHANNELS // 16, TONES // 2 * 8, 256), bf16),
            pltpu.VMEM((CHANNELS, CHANNELS), jnp.float32),
            pltpu.VMEM((2, LAGS, 16, CHANNELS), bf16),
            pltpu.SemaphoreType.DMA((5,)),
            pltpu.SemaphoreType.DMA((PARTS,)),
            pltpu.SemaphoreType.DMA((2,)),
        ],
        compiler_params=pltpu.CompilerParams(vmem_limit_bytes=56 * 2**20),
    )(right_table, lag_table, left_tones, flat, near, far)


def per_device(spectra, plan):
    left_table, right_table = (jnp.asarray(table, jnp.bfloat16) for table in window_tables())
    lag_table = jnp.asarray(lag_tables(), jnp.bfloat16)
    left_tones, flat, near, far = ring_move(plan, spectra.reshape(ROWS, BINS), left_table)
    return correlate(left_tones, flat, near, far, right_table, lag_table)[None, None]


def solution(mesh):
    in_specs = (P("ch", "seg", None, None, None), P(None, "ch"))
    out_specs = P("ch", "seg", None, None, None)
    return jax.shard_map(
        per_device, mesh=mesh, in_specs=in_specs, out_specs=out_specs, check_vma=False
    )
```

```python
import functools
import math

import jax
import jax.numpy as jnp
import numpy as np
from jax import lax
from jax.experimental import pallas as pl
from jax.experimental.pallas import tpu as pltpu
from jax.sharding import PartitionSpec as P

LAGS = 128
MESH = pl.DeviceIdType.MESH
RING = 8
CHUNKS = 4
SLOTS = 2 * CHUNKS
WIDTH = 2 * SLOTS + CHUNKS
STREAMS = 4
ROWS = 768
BLOCK = ROWS // CHUNKS
PIECE = BLOCK // STREAMS


def ring_plan():
    sends, lands = {}, {}

    def travel(mask, place, direction, chunk, slots):
        for hop, slot in enumerate(slots):
            at = (mask, (place + (hop if direction == 0 else -hop)) % RING, slot, direction)
            assert at not in sends and slot < SLOTS
            sends[at] = ("own", chunk) if hop == 0 else ("pass", slots[hop - 1])
        lands[mask, place ^ mask, chunk] = (direction, slots[-1])

    for mask in range(1, RING):
        for place in range(RING):
            ahead = ((place ^ mask) - place) % RING
            direction, hops = (0, ahead) if ahead <= 4 else (1, RING - ahead)
            for chunk in range(CHUNKS):
                go, rest = (0, 1, 3, 5)[chunk], (2, 4, 6, 7)[chunk]
                if mask == 4:
                    travel(mask, place, chunk % 2, chunk, [4 * (chunk // 2) + hop for hop in range(4)])
                elif mask in (3, 7):
                    travel(mask, place, direction, chunk, [go, go + 1, go + 2] if hops == 3 else [(0, 3, 5, 7)[chunk]])
                else:
                    travel(mask, place, direction, chunk, [[go], [go, rest], [go, go + 1, rest]][hops - 1])

    sources = [
        [sorted({what for at, what in sends.items() if at[2:] == (slot, way)}) for way in range(2)] for slot in range(SLOTS)
    ]
    spots = [sorted({where for at, where in lands.items() if at[2] == chunk}) + [None] for chunk in range(CHUNKS)]
    table = np.zeros((RING, RING, WIDTH), np.int32)
    for (mask, place, slot, way), what in sends.items():
        table[mask, place, slot * 2 + way] = sources[slot][way].index(what)
    for chunk in range(CHUNKS):
        for mask in range(RING):
            for place in range(RING):
                table[mask, place, 2 * SLOTS + chunk] = spots[chunk].index(lands.get((mask, place, chunk)))
    return sources, spots, table.reshape(-1)


SOURCES, SPOTS, CODES = ring_plan()
BINS = 512
SEGMENTS = 6
CHANNELS = 128
WINDOWS = 8
TONES = 128
SPAN = 2 * TONES
STEP = 256
UNROLL = 16
PARTS = TONES * 16 // STEP


def sixth(near, far, segment, part):
    first = (segment % 3) * 2 * CHANNELS + part * CHANNELS
    return (near if segment < 3 else far)[first:first + CHANNELS, :]


def lay_out(near, far, turned, segments):
    for segment in segments:
        lanes = slice(segment * CHANNELS, (segment + 1) * CHANNELS)
        for part in range(2):
            turned[part * BINS:(part + 1) * BINS, lanes] = sixth(near, far, segment, part).T


def ring_kernel(plan_in, table_in, left_table, mine_in, tones_out, flat_out, near_out, far_out, first, middle, beside, across,
                opposite, chosen, swapped, landed, staged, left_rows, left_turned, left_tones, flat, send_sem, recv_sem, x_send,
                x_recv, load_sem, store_sem, plan_ref, table_ref, mine_ref):
    load = pltpu.make_async_copy(left_table, left_rows, load_sem.at[0])
    early = [
        pltpu.make_async_copy(source, goal, load_sem.at[number])
        for number, (source, goal) in enumerate([(mine_in, mine_ref), (plan_in, plan_ref), (table_in, table_ref)], 1)
    ]
    for copy in early:
        copy.start()
    ch, seg = lax.axis_index("ch"), lax.axis_index("seg")
    z, y = ch // 2 % RING, ch // 32
    turned = ch + 16 - ch // 16 % 2 * 32
    targets = [
        ((ch + 32) % 256, seg),
        ((ch + 224) % 256, seg),
        (ch - z * 2 + (z + 1) % RING * 2, seg),
        (ch - z * 2 + (z + RING - 1) % RING * 2, seg),
        (turned, seg),
        (turned, 1 - seg),
        (ch + 1 - ch % 2 * 2, seg),
    ]
    barrier = pltpu.get_barrier_semaphore()
    for target in targets:
        pl.semaphore_signal(barrier, inc=1, device_id=target, device_id_type=MESH)
    pl.semaphore_wait(barrier, len(targets))

    def rows(start, count):
        return pl.ds(pl.multiple_of(start, 16), count)

    def x_copy(kind, chunk):
        all_rows = rows(chunk * BLOCK, BLOCK)
        upper, lower = rows(chunk * BLOCK, BLOCK // 2), rows(chunk * BLOCK + BLOCK // 2, BLOCK // 2)
        source, goal, target = [
            (mine_in.at[all_rows, :], beside.at[all_rows, :], targets[4]),
            (mine_in.at[all_rows, :], across.at[all_rows, :], targets[5]),
            (beside.at[upper, :], opposite.at[upper, :], targets[5]),
            (across.at[lower, :], opposite.at[lower, :], targets[4]),
            (chosen.at[0, all_rows, :], swapped.at[0, all_rows, :], targets[6]),
            (chosen.at[1, all_rows, :], swapped.at[1, all_rows, :], targets[6]),
        ][kind]
        return pltpu.make_async_remote_copy(
            src_ref=source,
            dst_ref=goal,
            send_sem=x_send.at[kind, chunk],
            recv_sem=x_recv.at[kind, chunk],
            device_id=target,
            device_id_type=MESH,
        )

    def spread(chunk):
        for kind in (0, 1):
            x_copy(kind, chunk).start()

    def forward(chunk):
        for kind in (0, 1):
            x_copy(kind, chunk).wait_recv()
        for kind in (2, 3):
            x_copy(kind, chunk).start()

    def choose(chunk):
        for kind in (2, 3):
            x_copy(kind, chunk).wait_recv()
        here = rows(chunk * BLOCK, BLOCK)
        chosen[0, here, :] = jnp.where(x_bit == 1, beside[here, :], mine_ref[here, :])
        chosen[1, here, :] = jnp.where(x_bit == 1, across[here, :], opposite[here, :])
        for kind in (4, 5):
            x_copy(kind, chunk).start()

    def settle(chunk):
        here = rows(chunk * BLOCK, BLOCK)
        for half in range(2):
            x_copy(4 + half, chunk).wait_recv()
            first[half, here, :] = jnp.where(core_bit == 1, swapped[half, here, :], chosen[half, here, :])

    def finish(chunk):
        for kind in range(6):
            x_copy(kind, chunk).wait_send()

    def store(number):
        where = pl.ds(number * (STEP // 16), STEP // 16)
        return pltpu.make_async_copy(left_tones.at[where], tones_out.at[where], store_sem.at[number])

    def left_part(number):
        part = rows(number * STEP, STEP)
        tones = jnp.dot(left_rows[part, :], left_turned[...], preferred_element_type=jnp.float32)
        for segment in range(SEGMENTS):
            piece_tones = tones[:, segment * CHANNELS:(segment + 1) * CHANNELS].reshape(STEP // 16, 16, CHANNELS)
            depth = slice(segment * 16, (segment + 1) * 16)
            left_tones[pl.ds(number * (STEP // 16), STEP // 16), depth, :] = piece_tones.astype(jnp.bfloat16)
        store(number).start()

    def flatten():
        first_lane = lax.broadcasted_iota(jnp.int32, (CHANNELS, 128), 1) == 0
        for segment in range(SEGMENTS):
            value = sixth(mine_ref, opposite, segment, 1)[:, :128].astype(jnp.float32)
            flat[segment * CHANNELS:(segment + 1) * CHANNELS, :] = jnp.where(first_lane, value, 0.0).astype(jnp.bfloat16)
        pltpu.make_async_copy(flat, flat_out, store_sem.at[PARTS]).start()

    spread(0)
    spread(1)
    load.start()
    for copy in early:
        copy.wait()
    mask = plan_ref[0, seg] ^ ch
    bases = [(((mask // 32) % RING) * RING + y) * WIDTH, (((mask // 2) % RING) * RING + z) * WIDTH]
    x_bit, core_bit = mask // 16 % 2, mask % 2
    forward(0)
    forward(1)
    spread(2)
    choose(0)
    settle(0)
    choose(1)
    spread(3)
    settle(1)

    def beside_slot(stage, slot):
        if stage == 0:
            if slot == 0:
                forward(2)
            elif slot == 1:
                choose(2)
                forward(3)
            elif slot == 2:
                settle(2)
                choose(3)
            elif slot == 3:
                settle(3)
                lay_out(mine_ref, opposite, left_turned, range(3))
            elif slot == 4:
                lay_out(mine_ref, opposite, left_turned, range(3, 6))
                flatten()
            elif slot == 5:
                load.wait()
            if slot >= 6:
                left_part(slot - 6)
        elif slot < 6:
            left_part(slot + 2)

    def ring_copy(stage, link, stream, slot):
        return pltpu.make_async_remote_copy(
            src_ref=staged.at[link, stream, slot % 2],
            dst_ref=landed.at[stage, link, stream, slot],
            send_sem=send_sem.at[link, stream, slot % 2],
            recv_sem=recv_sem.at[stage, link, stream, slot],
            device_id=targets[link],
            device_id_type=MESH,
        )

    def piece(stream, chunk):
        return rows(chunk * BLOCK + stream * PIECE, PIECE)

    def each_stream(body):
        def step(stream, carry):
            body(stream)
            return carry

        lax.fori_loop(0, STREAMS, step, 0)

    def send(stage, slot, source):
        def one(stream):
            for dim in range(2):
                for way in range(2):
                    link = 2 * dim + way
                    if slot >= 1:
                        ring_copy(stage, link, stream, slot - 1).wait_recv()
                    if slot >= 2:
                        ring_copy(stage, link, stream, slot - 2).wait_send()
                    code = table_ref[bases[dim] + slot * 2 + way]
                    value = None
                    for number, (kind, index) in enumerate(SOURCES[slot][way]):
                        if kind == "own":
                            option = source[dim ^ stage][piece(stream, index), :]
                        else:
                            option = landed[stage, link, stream, index]
                        value = option if value is None else jnp.where(code == number, option, value)
                    staged[link, stream, slot % 2] = value
                    ring_copy(stage, link, stream, slot).start()

        each_stream(one)

    def pick(stage, chunk, source, goal):
        def one(stream):
            for dim in range(2):
                code = table_ref[bases[dim] + 2 * SLOTS + chunk]
                value = source[dim ^ stage][piece(stream, chunk), :]
                for number, spot in enumerate(SPOTS[chunk][:-1]):
                    value = jnp.where(code == number, landed[stage, 2 * dim + spot[0], stream, spot[1]], value)
                goal[dim ^ stage][piece(stream, chunk), :] = value

        each_stream(one)

    def drain(stage):
        def one(stream):
            for link in range(4):
                ring_copy(stage, link, stream, SLOTS - 1).wait_recv()
                ring_copy(stage, link, stream, SLOTS - 2).wait_send()
                ring_copy(stage, link, stream, SLOTS - 1).wait_send()

        each_stream(one)

    last = [max(spot[1] for spot in spots[:-1]) for spots in SPOTS]
    sides = [(first.at[0], first.at[1]), (middle.at[0], middle.at[1]), (near_out, far_out)]
    late = []
    for stage in range(2):
        source, goal = sides[stage], sides[stage + 1]
        for slot in range(SLOTS):
            send(stage, slot, source)
            for chunk in late:
                pick(0, chunk, sides[0], sides[1])
            late = []
            for chunk in range(CHUNKS):
                if last[chunk] == slot - 1:
                    pick(stage, chunk, source, goal)
            beside_slot(stage, slot)
        drain(stage)
        rest = [chunk for chunk in range(CHUNKS) if last[chunk] == SLOTS - 1]
        if stage == 0:
            late = [chunk for chunk in rest if chunk >= 2]
        for chunk in rest:
            if chunk not in late:
                pick(stage, chunk, source, goal)

    for chunk in range(CHUNKS):
        finish(chunk)
    for number in range(PARTS):
        store(number).wait()
    pltpu.make_async_copy(flat, flat_out, store_sem.at[PARTS]).wait()


def ring_move(plan, mine, left_table):
    width = mine.shape[-1]
    vmem = pl.BlockSpec(memory_space=pltpu.VMEM)
    hbm = pl.BlockSpec(memory_space=pl.ANY)
    bf16 = jnp.bfloat16
    return pl.pallas_call(
        ring_kernel,
        out_shape=[
            jax.ShapeDtypeStruct((TONES, SEGMENTS * 16, CHANNELS), bf16),
            jax.ShapeDtypeStruct((SEGMENTS * CHANNELS, 128), bf16),
            jax.ShapeDtypeStruct((ROWS, width), bf16),
            jax.ShapeDtypeStruct((ROWS, width), bf16),
        ],
        in_specs=[hbm] * 4,
        out_specs=[hbm, hbm, vmem, vmem],
        scratch_shapes=[
            pltpu.VMEM((2, ROWS, width), bf16),
            pltpu.VMEM((2, ROWS, width), bf16),
            pltpu.VMEM((ROWS, width), bf16),
            pltpu.VMEM((ROWS, width), bf16),
            pltpu.VMEM((ROWS, width), bf16),
            pltpu.VMEM((2, ROWS, width), bf16),
            pltpu.VMEM((2, ROWS, width), bf16),
            pltpu.VMEM((2, 4, STREAMS, SLOTS, PIECE, width), bf16),
            pltpu.VMEM((4, STREAMS, 2, PIECE, width), bf16),
            pltpu.VMEM((TONES * 16, 2 * BINS), bf16),
            pltpu.VMEM((2 * BINS, SEGMENTS * CHANNELS), bf16),
            pltpu.VMEM((TONES, SEGMENTS * 16, CHANNELS), bf16),
            pltpu.VMEM((SEGMENTS * CHANNELS, 128), bf16),
            pltpu.SemaphoreType.DMA((4, STREAMS, 2)),
            pltpu.SemaphoreType.DMA((2, 4, STREAMS, SLOTS)),
            pltpu.SemaphoreType.DMA((6, CHUNKS)),
            pltpu.SemaphoreType.DMA((6, CHUNKS)),
            pltpu.SemaphoreType.DMA((4,)),
            pltpu.SemaphoreType.DMA((PARTS + 1,)),
            pltpu.SMEM((1, plan.shape[0]), jnp.int32),
            pltpu.SMEM(CODES.shape, jnp.int32),
            pltpu.VMEM((ROWS, width), bf16),
        ],
        compiler_params=pltpu.CompilerParams(
            collective_id=0, has_side_effects=True, vmem_limit_bytes=56 * 2**20
        ),
    )(plan.T, jnp.asarray(CODES), left_table, mine)


def window_tables():
    time = np.arange(1024)
    bins = np.arange(BINS)
    angle = 2 * np.pi * (np.outer(time, bins) % 1024) / 1024
    weight = np.where(bins == 0, np.sqrt(0.5), 1.0)
    samples = np.concatenate([np.cos(angle) * weight, -np.sin(angle) * weight], axis=1)
    tones = 2 * np.pi * (np.arange(TONES) + 0.5) / SPAN

    def table(offsets):
        turn = np.exp(-1j * np.outer(tones, offsets))
        result = np.empty((TONES, 2, WINDOWS, 2 * BINS))
        for window in range(WINDOWS):
            both = turn @ samples[(window * 128 + offsets) % 1024]
            result[:, 0, window], result[:, 1, window] = both.real, both.imag
        return (result / 32.0).reshape(TONES * 2 * WINDOWS, 2 * BINS)

    return table(np.arange(-64, 192)), table(np.arange(128))


def lag_tables():
    tones = 2 * np.pi * (np.arange(TONES // 2) + 0.5) / SPAN
    scale = 1024.0 / BINS * 2.0 / SPAN / math.sqrt(2.0 * SEGMENTS * BINS)
    even, late, odd = np.arange(0, 65, 2), np.arange(2, 65, 2), np.arange(1, 64, 2)
    parts = [np.cos(np.outer(even, tones)), np.sin(np.outer(late, tones))]
    parts += [np.cos(np.outer(odd, tones)), np.sin(np.outer(odd, tones))]
    return np.kron(np.concatenate(parts, axis=0) * scale, np.eye(8))


def correlate_kernel(right_table, lag_table, left_ref, flat_ref, near_ref, far_ref, out_ref,
                     right_rows, lag_rows, left_tones, flat, near, far, right_turned, right_tones, folded, constant, held,
                     load_sem, part_sem, out_sem):
    f32, bf16 = jnp.float32, jnp.bfloat16
    loads = [
        pltpu.make_async_copy(source, goal, load_sem.at[number])
        for number, (source, goal) in enumerate(
            [(near_ref, near), (far_ref, far), (flat_ref, flat), (left_ref, left_tones), (lag_table, lag_rows)]
        )
    ]

    def part_rows(number):
        return pl.ds(pl.multiple_of(number * STEP, STEP), STEP)

    def part_load(number):
        rows = part_rows(number)
        return pltpu.make_async_copy(right_table.at[rows, :], right_rows.at[rows, :], part_sem.at[number])

    def result(pair):
        rows = pl.ds(pl.multiple_of(pair * 16, 16), 16)
        return pltpu.make_async_copy(held.at[pair % 2], out_ref.at[:, rows, :], out_sem.at[pair % 2])

    for load in loads[:2]:
        load.start()
    for number in range(2):
        part_load(number).start()

    loads[0].wait()
    lay_out(near, far, right_turned, range(3))
    loads[1].wait()
    for number in range(2, PARTS):
        part_load(number).start()
    for load in loads[2:]:
        load.start()
    lay_out(near, far, right_turned, range(3, 6))

    def tones_of(number, carry):
        part_load(number).wait()
        where = pl.ds(number * (STEP // 16), STEP // 16)
        right = jnp.dot(right_rows[part_rows(number), :], right_turned[...], preferred_element_type=f32)
        for segment in range(SEGMENTS):
            lanes = slice(segment * CHANNELS, (segment + 1) * CHANNELS)
            depth = slice(segment * 16, (segment + 1) * 16)
            plain = right[:, lanes].reshape(STEP // 16, 2, 8, CHANNELS)
            right_tones[where, depth, :CHANNELS] = plain.reshape(STEP // 16, 16, CHANNELS).astype(bf16)
            turned = jnp.concatenate([-plain[:, 1], plain[:, 0]], axis=1)
            right_tones[where, depth, CHANNELS:] = turned.astype(bf16)
        return carry

    lax.fori_loop(0, PARTS, tones_of, 0)

    loads[2].wait()
    total = jnp.zeros((CHANNELS, CHANNELS), f32)
    for segment in range(SEGMENTS):
        mine = flat[segment * CHANNELS:(segment + 1) * CHANNELS, :]
        theirs = sixth(near, far, segment, 1)[:, :128]
        total += lax.dot_general(mine, theirs, (((1,), (1,)), ((), ())), preferred_element_type=f32)
    constant[...] = total * (1.0 / math.sqrt(2.0 * SEGMENTS * BINS))
    loads[3].wait()

    def cross(tone):
        return jnp.dot(left_tones[tone].T, right_tones[tone], preferred_element_type=f32)

    def fold(number, carry):
        tone = number * 2
        pairs = []
        for offset in range(2):
            low, high = cross(tone + offset), cross(TONES - 1 - tone - offset)
            plus, minus = low + high, low - high
            pairs.append((plus[:, :128], minus[:, 128:], minus[:, :128], plus[:, 128:]))
        rows = pl.ds(pl.multiple_of(number * 16, 16), 16)
        for kind in range(4):
            one, two = pairs[0][kind], pairs[1][kind]
            for group in range(16):
                both = jnp.concatenate([one[group * 8:group * 8 + 8], two[group * 8:group * 8 + 8]], axis=0)
                lanes = slice((group % 2) * 128, (group % 2) * 128 + 128)
                folded[kind, group // 2, rows, lanes] = both.astype(bf16)
        return carry

    lax.fori_loop(0, TONES // 4, fold, 0, unroll=UNROLL)
    loads[4].wait()

    def lags(pair, carry):
        slot = pair % 2
        base = constant[pl.ds(pl.multiple_of(pair * 16, 16), 16), :]

        @pl.when(pair >= 2)
        def _():
            result(pair - 2).wait()

        def turn(kind, first, count):
            both = jnp.dot(lag_rows[first * 8:(first + count) * 8, :], folded[kind, pair], preferred_element_type=f32)
            both = both.reshape(count, 8, 256)
            return jnp.concatenate([both[:, :, :128], both[:, :, 128:]], axis=1)

        cosines, sines = turn(0, 0, 33) + base, turn(1, 33, 32)
        held[slot, 64, :, :] = cosines[0].astype(bf16)
        for lag in range(1, 33):
            if lag < 32:
                held[slot, 64 + 2 * lag, :, :] = (cosines[lag] - sines[lag - 1]).astype(bf16)
            held[slot, 64 - 2 * lag, :, :] = (cosines[lag] + sines[lag - 1]).astype(bf16)
        cosines, sines = turn(2, 65, 32) + base, turn(3, 97, 32)
        for lag in range(32):
            held[slot, 65 + 2 * lag, :, :] = (cosines[lag] - sines[lag]).astype(bf16)
            held[slot, 63 - 2 * lag, :, :] = (cosines[lag] + sines[lag]).astype(bf16)
        result(pair).start()
        return carry

    lax.fori_loop(0, CHANNELS // 16, lags, 0)
    result(CHANNELS // 16 - 2).wait()
    result(CHANNELS // 16 - 1).wait()


def correlate(left_tones, flat, near, far, right_table, lag_table):
    hbm = pl.BlockSpec(memory_space=pl.ANY)
    bf16 = jnp.bfloat16
    return pl.pallas_call(
        correlate_kernel,
        out_shape=jax.ShapeDtypeStruct((LAGS, CHANNELS, CHANNELS), bf16),
        in_specs=[hbm] * 6,
        out_specs=hbm,
        scratch_shapes=[
            pltpu.VMEM(right_table.shape, bf16),
            pltpu.VMEM(lag_table.shape, bf16),
            pltpu.VMEM(left_tones.shape, bf16),
            pltpu.VMEM(flat.shape, bf16),
            pltpu.VMEM(near.shape, bf16),
            pltpu.VMEM(far.shape, bf16),
            pltpu.VMEM((2 * BINS, SEGMENTS * CHANNELS), bf16),
            pltpu.VMEM((TONES, SEGMENTS * 16, 2 * CHANNELS), bf16),
            pltpu.VMEM((4, CHANNELS // 16, TONES // 2 * 8, 256), bf16),
            pltpu.VMEM((CHANNELS, CHANNELS), jnp.float32),
            pltpu.VMEM((2, LAGS, 16, CHANNELS), bf16),
            pltpu.SemaphoreType.DMA((5,)),
            pltpu.SemaphoreType.DMA((PARTS,)),
            pltpu.SemaphoreType.DMA((2,)),
        ],
        compiler_params=pltpu.CompilerParams(vmem_limit_bytes=56 * 2**20),
    )(right_table, lag_table, left_tones, flat, near, far)


def per_device(spectra, plan):
    left_table, right_table = (jnp.asarray(table, jnp.bfloat16) for table in window_tables())
    lag_table = jnp.asarray(lag_tables(), jnp.bfloat16)
    left_tones, flat, near, far = ring_move(plan, spectra.reshape(ROWS, BINS), left_table)
    return correlate(left_tones, flat, near, far, right_table, lag_table)[None, None]


def solution(mesh):
    in_specs = (P("ch", "seg", None, None, None), P(None, "ch"))
    out_specs = P("ch", "seg", None, None, None)
    return jax.shard_map(
        per_device, mesh=mesh, in_specs=in_specs, out_specs=out_specs, check_vma=False
    )
```

```python
import functools
import math

import jax
import jax.numpy as jnp
import numpy as np
from jax import lax
from jax.experimental import pallas as pl
from jax.experimental.pallas import tpu as pltpu
from jax.sharding import PartitionSpec as P

LAGS = 128
MESH = pl.DeviceIdType.MESH
RING = 8
CHUNKS = 4
SLOTS = 2 * CHUNKS
WIDTH = 2 * SLOTS + CHUNKS
STREAMS = 4
ROWS = 768
BLOCK = ROWS // CHUNKS
PIECE = BLOCK // STREAMS


def ring_plan():
    sends, lands = {}, {}

    def travel(mask, place, direction, chunk, slots):
        for hop, slot in enumerate(slots):
            at = (mask, (place + (hop if direction == 0 else -hop)) % RING, slot, direction)
            assert at not in sends and slot < SLOTS
            sends[at] = ("own", chunk) if hop == 0 else ("pass", slots[hop - 1])
        lands[mask, place ^ mask, chunk] = (direction, slots[-1])

    for mask in range(1, RING):
        for place in range(RING):
            ahead = ((place ^ mask) - place) % RING
            direction, hops = (0, ahead) if ahead <= 4 else (1, RING - ahead)
            for chunk in range(CHUNKS):
                go, rest = (0, 1, 3, 5)[chunk], (2, 4, 6, 7)[chunk]
                if mask == 4:
                    travel(mask, place, chunk % 2, chunk, [4 * (chunk // 2) + hop for hop in range(4)])
                elif mask in (3, 7):
                    travel(mask, place, direction, chunk, [go, go + 1, go + 2] if hops == 3 else [(0, 3, 5, 7)[chunk]])
                else:
                    travel(mask, place, direction, chunk, [[go], [go, rest], [go, go + 1, rest]][hops - 1])

    sources = [
        [sorted({what for at, what in sends.items() if at[2:] == (slot, way)}) for way in range(2)] for slot in range(SLOTS)
    ]
    spots = [sorted({where for at, where in lands.items() if at[2] == chunk}) + [None] for chunk in range(CHUNKS)]
    table = np.zeros((RING, RING, WIDTH), np.int32)
    for (mask, place, slot, way), what in sends.items():
        table[mask, place, slot * 2 + way] = sources[slot][way].index(what)
    for chunk in range(CHUNKS):
        for mask in range(RING):
            for place in range(RING):
                table[mask, place, 2 * SLOTS + chunk] = spots[chunk].index(lands.get((mask, place, chunk)))
    return sources, spots, table.reshape(-1)


SOURCES, SPOTS, CODES = ring_plan()
BINS = 512
SEGMENTS = 6
CHANNELS = 128
WINDOWS = 8
TONES = 128
SPAN = 2 * TONES
STEP = 256
UNROLL = 16
PARTS = TONES * 16 // STEP


def sixth(near, far, segment, part):
    first = (segment % 3) * 2 * CHANNELS + part * CHANNELS
    return (near if segment < 3 else far)[first:first + CHANNELS, :]


def lay_out(near, far, turned, segments):
    for segment in segments:
        lanes = slice(segment * CHANNELS, (segment + 1) * CHANNELS)
        for part in range(2):
            turned[part * BINS:(part + 1) * BINS, lanes] = sixth(near, far, segment, part).T


def ring_kernel(plan_in, table_in, left_table, mine_in, tones_out, flat_out, near_out, far_out, first, middle, beside, across,
                opposite, chosen, swapped, landed, staged, left_rows, left_turned, left_tones, flat, send_sem, recv_sem, x_send,
                x_recv, load_sem, store_sem, plan_ref, table_ref, mine_ref, last_half, out_sem):
    load = pltpu.make_async_copy(left_table, left_rows, load_sem.at[0])
    early = [
        pltpu.make_async_copy(source, goal, load_sem.at[number])
        for number, (source, goal) in enumerate([(mine_in, mine_ref), (plan_in, plan_ref), (table_in, table_ref)], 1)
    ]
    for copy in early:
        copy.start()
    ch, seg = lax.axis_index("ch"), lax.axis_index("seg")
    z, y = ch // 2 % RING, ch // 32
    turned = ch + 16 - ch // 16 % 2 * 32
    targets = [
        ((ch + 32) % 256, seg),
        ((ch + 224) % 256, seg),
        (ch - z * 2 + (z + 1) % RING * 2, seg),
        (ch - z * 2 + (z + RING - 1) % RING * 2, seg),
        (turned, seg),
        (turned, 1 - seg),
        (ch + 1 - ch % 2 * 2, seg),
    ]
    barrier = pltpu.get_barrier_semaphore()
    for target in targets:
        pl.semaphore_signal(barrier, inc=1, device_id=target, device_id_type=MESH)
    pl.semaphore_wait(barrier, len(targets))

    def rows(start, count):
        return pl.ds(pl.multiple_of(start, 16), count)

    def x_copy(kind, chunk):
        all_rows = rows(chunk * BLOCK, BLOCK)
        upper, lower = rows(chunk * BLOCK, BLOCK // 2), rows(chunk * BLOCK + BLOCK // 2, BLOCK // 2)
        source, goal, target = [
            (mine_in.at[all_rows, :], beside.at[all_rows, :], targets[4]),
            (mine_in.at[all_rows, :], across.at[all_rows, :], targets[5]),
            (beside.at[upper, :], opposite.at[upper, :], targets[5]),
            (across.at[lower, :], opposite.at[lower, :], targets[4]),
            (chosen.at[0, all_rows, :], swapped.at[0, all_rows, :], targets[6]),
            (chosen.at[1, all_rows, :], swapped.at[1, all_rows, :], targets[6]),
        ][kind]
        return pltpu.make_async_remote_copy(
            src_ref=source,
            dst_ref=goal,
            send_sem=x_send.at[kind, chunk],
            recv_sem=x_recv.at[kind, chunk],
            device_id=target,
            device_id_type=MESH,
        )

    def spread(chunk):
        for kind in (0, 1):
            x_copy(kind, chunk).start()

    def forward(chunk):
        for kind in (0, 1):
            x_copy(kind, chunk).wait_recv()
        for kind in (2, 3):
            x_copy(kind, chunk).start()

    def choose(chunk):
        for kind in (2, 3):
            x_copy(kind, chunk).wait_recv()
        here = rows(chunk * BLOCK, BLOCK)
        chosen[0, here, :] = jnp.where(x_bit == 1, beside[here, :], mine_ref[here, :])
        chosen[1, here, :] = jnp.where(x_bit == 1, across[here, :], opposite[here, :])
        for kind in (4, 5):
            x_copy(kind, chunk).start()

    def settle(chunk):
        here = rows(chunk * BLOCK, BLOCK)
        for half in range(2):
            x_copy(4 + half, chunk).wait_recv()
            first[half, here, :] = jnp.where(core_bit == 1, swapped[half, here, :], chosen[half, here, :])

    def finish(chunk):
        for kind in range(6):
            x_copy(kind, chunk).wait_send()

    def store(number):
        where = pl.ds(number * (STEP // 16), STEP // 16)
        return pltpu.make_async_copy(left_tones.at[where], tones_out.at[where], store_sem.at[number])

    def left_part(number):
        part = rows(number * STEP, STEP)
        tones = jnp.dot(left_rows[part, :], left_turned[...], preferred_element_type=jnp.float32)
        for segment in range(SEGMENTS):
            piece_tones = tones[:, segment * CHANNELS:(segment + 1) * CHANNELS].reshape(STEP // 16, 16, CHANNELS)
            depth = slice(segment * 16, (segment + 1) * 16)
            left_tones[pl.ds(number * (STEP // 16), STEP // 16), depth, :] = piece_tones.astype(jnp.bfloat16)
        store(number).start()

    def flatten():
        first_lane = lax.broadcasted_iota(jnp.int32, (CHANNELS, 128), 1) == 0
        for segment in range(SEGMENTS):
            value = sixth(mine_ref, opposite, segment, 1)[:, :128].astype(jnp.float32)
            flat[segment * CHANNELS:(segment + 1) * CHANNELS, :] = jnp.where(first_lane, value, 0.0).astype(jnp.bfloat16)
        pltpu.make_async_copy(flat, flat_out, store_sem.at[PARTS]).start()

    spread(0)
    spread(1)
    load.start()
    for copy in early:
        copy.wait()
    mask = plan_ref[0, seg] ^ ch
    bases = [(((mask // 32) % RING) * RING + y) * WIDTH, (((mask // 2) % RING) * RING + z) * WIDTH]
    x_bit, core_bit = mask // 16 % 2, mask % 2
    forward(0)
    forward(1)
    spread(2)
    choose(0)
    settle(0)
    choose(1)
    spread(3)
    settle(1)

    def beside_slot(stage, slot):
        if stage == 0:
            if slot == 0:
                forward(2)
            elif slot == 1:
                choose(2)
                forward(3)
            elif slot == 2:
                settle(2)
                choose(3)
            elif slot == 3:
                settle(3)
                lay_out(mine_ref, opposite, left_turned, range(3))
            elif slot == 4:
                lay_out(mine_ref, opposite, left_turned, range(3, 6))
                flatten()
            elif slot == 5:
                load.wait()
            if slot >= 6:
                left_part(slot - 6)
        elif slot < 6:
            left_part(slot + 2)

    def ring_copy(stage, link, stream, slot):
        return pltpu.make_async_remote_copy(
            src_ref=staged.at[link, stream, slot % 2],
            dst_ref=landed.at[stage, link, stream, slot],
            send_sem=send_sem.at[link, stream, slot % 2],
            recv_sem=recv_sem.at[stage, link, stream, slot],
            device_id=targets[link],
            device_id_type=MESH,
        )

    def piece(stream, chunk):
        return rows(chunk * BLOCK + stream * PIECE, PIECE)

    def each_stream(body):
        def step(stream, carry):
            body(stream)
            return carry

        lax.fori_loop(0, STREAMS, step, 0)

    def send(stage, slot, source):
        def one(stream):
            for dim in range(2):
                for way in range(2):
                    link = 2 * dim + way
                    if slot >= 1:
                        ring_copy(stage, link, stream, slot - 1).wait_recv()
                    if slot >= 2:
                        ring_copy(stage, link, stream, slot - 2).wait_send()
                    code = table_ref[bases[dim] + slot * 2 + way]
                    value = None
                    for number, (kind, index) in enumerate(SOURCES[slot][way]):
                        if kind == "own":
                            option = source[dim ^ stage][piece(stream, index), :]
                        else:
                            option = landed[stage, link, stream, index]
                        value = option if value is None else jnp.where(code == number, option, value)
                    staged[link, stream, slot % 2] = value
                    ring_copy(stage, link, stream, slot).start()

        each_stream(one)

    def pick(stage, chunk, source, goal):
        def one(stream):
            for dim in range(2):
                code = table_ref[bases[dim] + 2 * SLOTS + chunk]
                value = source[dim ^ stage][piece(stream, chunk), :]
                for number, spot in enumerate(SPOTS[chunk][:-1]):
                    value = jnp.where(code == number, landed[stage, 2 * dim + spot[0], stream, spot[1]], value)
                goal[dim ^ stage][piece(stream, chunk), :] = value

        each_stream(one)
        if stage == 1:
            for copy in give(chunk):
                copy.start()

    def give(chunk):
        here = rows(chunk * BLOCK, BLOCK)
        return [
            pltpu.make_async_copy(last_half.at[half, here, :], goal.at[here, :], out_sem.at[half, chunk])
            for half, goal in enumerate((near_out, far_out))
        ]

    def drain(stage):
        def one(stream):
            for link in range(4):
                ring_copy(stage, link, stream, SLOTS - 1).wait_recv()
                ring_copy(stage, link, stream, SLOTS - 2).wait_send()
                ring_copy(stage, link, stream, SLOTS - 1).wait_send()

        each_stream(one)

    last = [max(spot[1] for spot in spots[:-1]) for spots in SPOTS]
    sides = [(first.at[0], first.at[1]), (middle.at[0], middle.at[1]), (last_half.at[0], last_half.at[1])]
    late = []
    for stage in range(2):
        source, goal = sides[stage], sides[stage + 1]
        for slot in range(SLOTS):
            send(stage, slot, source)
            for chunk in late:
                pick(0, chunk, sides[0], sides[1])
            late = []
            for chunk in range(CHUNKS):
                if last[chunk] == slot - 1:
                    pick(stage, chunk, source, goal)
            beside_slot(stage, slot)
        drain(stage)
        rest = [chunk for chunk in range(CHUNKS) if last[chunk] == SLOTS - 1]
        if stage == 0:
            late = [chunk for chunk in rest if chunk >= 2]
        for chunk in rest:
            if chunk not in late:
                pick(stage, chunk, source, goal)

    for chunk in range(CHUNKS):
        finish(chunk)
    for number in range(PARTS):
        store(number).wait()
    for chunk in range(CHUNKS):
        for copy in give(chunk):
            copy.wait()
    pltpu.make_async_copy(flat, flat_out, store_sem.at[PARTS]).wait()


def ring_move(plan, mine, left_table):
    width = mine.shape[-1]
    hbm = pl.BlockSpec(memory_space=pl.ANY)
    bf16 = jnp.bfloat16
    return pl.pallas_call(
        ring_kernel,
        out_shape=[
            jax.ShapeDtypeStruct((TONES, SEGMENTS * 16, CHANNELS), bf16),
            jax.ShapeDtypeStruct((SEGMENTS * CHANNELS, 128), bf16),
            jax.ShapeDtypeStruct((ROWS, width), bf16),
            jax.ShapeDtypeStruct((ROWS, width), bf16),
        ],
        in_specs=[hbm] * 4,
        out_specs=[hbm] * 4,
        scratch_shapes=[
            pltpu.VMEM((2, ROWS, width), bf16),
            pltpu.VMEM((2, ROWS, width), bf16),
            pltpu.VMEM((ROWS, width), bf16),
            pltpu.VMEM((ROWS, width), bf16),
            pltpu.VMEM((ROWS, width), bf16),
            pltpu.VMEM((2, ROWS, width), bf16),
            pltpu.VMEM((2, ROWS, width), bf16),
            pltpu.VMEM((2, 4, STREAMS, SLOTS, PIECE, width), bf16),
            pltpu.VMEM((4, STREAMS, 2, PIECE, width), bf16),
            pltpu.VMEM((TONES * 16, 2 * BINS), bf16),
            pltpu.VMEM((2 * BINS, SEGMENTS * CHANNELS), bf16),
            pltpu.VMEM((TONES, SEGMENTS * 16, CHANNELS), bf16),
            pltpu.VMEM((SEGMENTS * CHANNELS, 128), bf16),
            pltpu.SemaphoreType.DMA((4, STREAMS, 2)),
            pltpu.SemaphoreType.DMA((2, 4, STREAMS, SLOTS)),
            pltpu.SemaphoreType.DMA((6, CHUNKS)),
            pltpu.SemaphoreType.DMA((6, CHUNKS)),
            pltpu.SemaphoreType.DMA((4,)),
            pltpu.SemaphoreType.DMA((PARTS + 1,)),
            pltpu.SMEM((1, plan.shape[0]), jnp.int32),
            pltpu.SMEM(CODES.shape, jnp.int32),
            pltpu.VMEM((ROWS, width), bf16),
            pltpu.VMEM((2, ROWS, width), bf16),
            pltpu.SemaphoreType.DMA((2, CHUNKS)),
        ],
        compiler_params=pltpu.CompilerParams(
            collective_id=0, has_side_effects=True, vmem_limit_bytes=56 * 2**20
        ),
    )(plan.T, jnp.asarray(CODES), left_table, mine)


def window_tables():
    time = np.arange(1024)
    bins = np.arange(BINS)
    angle = 2 * np.pi * (np.outer(time, bins) % 1024) / 1024
    weight = np.where(bins == 0, np.sqrt(0.5), 1.0)
    samples = np.concatenate([np.cos(angle) * weight, -np.sin(angle) * weight], axis=1)
    tones = 2 * np.pi * (np.arange(TONES) + 0.5) / SPAN

    def table(offsets):
        turn = np.exp(-1j * np.outer(tones, offsets))
        result = np.empty((TONES, 2, WINDOWS, 2 * BINS))
        for window in range(WINDOWS):
            both = turn @ samples[(window * 128 + offsets) % 1024]
            result[:, 0, window], result[:, 1, window] = both.real, both.imag
        return (result / 32.0).reshape(TONES * 2 * WINDOWS, 2 * BINS)

    return table(np.arange(-64, 192)), table(np.arange(128))


def lag_tables():
    tones = 2 * np.pi * (np.arange(TONES // 2) + 0.5) / SPAN
    scale = 1024.0 / BINS * 2.0 / SPAN / math.sqrt(2.0 * SEGMENTS * BINS)
    even, late, odd = np.arange(0, 65, 2), np.arange(2, 65, 2), np.arange(1, 64, 2)
    parts = [np.cos(np.outer(even, tones)), np.sin(np.outer(late, tones))]
    parts += [np.cos(np.outer(odd, tones)), np.sin(np.outer(odd, tones))]
    return np.kron(np.concatenate(parts, axis=0) * scale, np.eye(8))


def correlate_kernel(right_table, lag_table, left_ref, flat_ref, near_ref, far_ref, out_ref,
                     right_rows, lag_rows, left_tones, flat, near, far, right_turned, right_tones, folded, constant, held,
                     load_sem, part_sem, out_sem):
    f32, bf16 = jnp.float32, jnp.bfloat16
    loads = [
        pltpu.make_async_copy(source, goal, load_sem.at[number])
        for number, (source, goal) in enumerate(
            [(near_ref, near), (far_ref, far), (flat_ref, flat), (left_ref, left_tones), (lag_table, lag_rows)]
        )
    ]

    def part_rows(number):
        return pl.ds(pl.multiple_of(number * STEP, STEP), STEP)

    def part_load(number):
        rows = part_rows(number)
        return pltpu.make_async_copy(right_table.at[rows, :], right_rows.at[rows, :], part_sem.at[number])

    def result(pair):
        rows = pl.ds(pl.multiple_of(pair * 16, 16), 16)
        return pltpu.make_async_copy(held.at[pair % 2], out_ref.at[:, rows, :], out_sem.at[pair % 2])

    for load in loads[:2]:
        load.start()
    for number in range(2):
        part_load(number).start()

    loads[0].wait()
    lay_out(near, far, right_turned, range(3))
    loads[1].wait()
    for number in range(2, PARTS):
        part_load(number).start()
    for load in loads[2:]:
        load.start()
    lay_out(near, far, right_turned, range(3, 6))

    def tones_of(number, carry):
        part_load(number).wait()
        where = pl.ds(number * (STEP // 16), STEP // 16)
        right = jnp.dot(right_rows[part_rows(number), :], right_turned[...], preferred_element_type=f32)
        for segment in range(SEGMENTS):
            lanes = slice(segment * CHANNELS, (segment + 1) * CHANNELS)
            depth = slice(segment * 16, (segment + 1) * 16)
            plain = right[:, lanes].reshape(STEP // 16, 2, 8, CHANNELS)
            right_tones[where, depth, :CHANNELS] = plain.reshape(STEP // 16, 16, CHANNELS).astype(bf16)
            turned = jnp.concatenate([-plain[:, 1], plain[:, 0]], axis=1)
            right_tones[where, depth, CHANNELS:] = turned.astype(bf16)
        return carry

    lax.fori_loop(0, PARTS, tones_of, 0)

    loads[2].wait()
    total = jnp.zeros((CHANNELS, CHANNELS), f32)
    for segment in range(SEGMENTS):
        mine = flat[segment * CHANNELS:(segment + 1) * CHANNELS, :]
        theirs = sixth(near, far, segment, 1)[:, :128]
        total += lax.dot_general(mine, theirs, (((1,), (1,)), ((), ())), preferred_element_type=f32)
    constant[...] = total * (1.0 / math.sqrt(2.0 * SEGMENTS * BINS))
    loads[3].wait()

    def cross(tone):
        return jnp.dot(left_tones[tone].T, right_tones[tone], preferred_element_type=f32)

    def fold(number, carry):
        tone = number * 2
        pairs = []
        for offset in range(2):
            low, high = cross(tone + offset), cross(TONES - 1 - tone - offset)
            plus, minus = low + high, low - high
            pairs.append((plus[:, :128], minus[:, 128:], minus[:, :128], plus[:, 128:]))
        rows = pl.ds(pl.multiple_of(number * 16, 16), 16)
        for kind in range(4):
            one, two = pairs[0][kind], pairs[1][kind]
            for group in range(16):
                both = jnp.concatenate([one[group * 8:group * 8 + 8], two[group * 8:group * 8 + 8]], axis=0)
                lanes = slice((group % 2) * 128, (group % 2) * 128 + 128)
                folded[kind, group // 2, rows, lanes] = both.astype(bf16)
        return carry

    lax.fori_loop(0, TONES // 4, fold, 0, unroll=UNROLL)
    loads[4].wait()

    def lags(pair, carry):
        slot = pair % 2
        base = constant[pl.ds(pl.multiple_of(pair * 16, 16), 16), :]

        @pl.when(pair >= 2)
        def _():
            result(pair - 2).wait()

        def turn(kind, first, count):
            both = jnp.dot(lag_rows[first * 8:(first + count) * 8, :], folded[kind, pair], preferred_element_type=f32)
            both = both.reshape(count, 8, 256)
            return jnp.concatenate([both[:, :, :128], both[:, :, 128:]], axis=1)

        cosines, sines = turn(0, 0, 33) + base, turn(1, 33, 32)
        held[slot, 64, :, :] = cosines[0].astype(bf16)
        for lag in range(1, 33):
            if lag < 32:
                held[slot, 64 + 2 * lag, :, :] = (cosines[lag] - sines[lag - 1]).astype(bf16)
            held[slot, 64 - 2 * lag, :, :] = (cosines[lag] + sines[lag - 1]).astype(bf16)
        cosines, sines = turn(2, 65, 32) + base, turn(3, 97, 32)
        for lag in range(32):
            held[slot, 65 + 2 * lag, :, :] = (cosines[lag] - sines[lag]).astype(bf16)
            held[slot, 63 - 2 * lag, :, :] = (cosines[lag] + sines[lag]).astype(bf16)
        result(pair).start()
        return carry

    lax.fori_loop(0, CHANNELS // 16, lags, 0)
    result(CHANNELS // 16 - 2).wait()
    result(CHANNELS // 16 - 1).wait()


def correlate(left_tones, flat, near, far, right_table, lag_table):
    hbm = pl.BlockSpec(memory_space=pl.ANY)
    bf16 = jnp.bfloat16
    return pl.pallas_call(
        correlate_kernel,
        out_shape=jax.ShapeDtypeStruct((LAGS, CHANNELS, CHANNELS), bf16),
        in_specs=[hbm] * 6,
        out_specs=hbm,
        scratch_shapes=[
            pltpu.VMEM(right_table.shape, bf16),
            pltpu.VMEM(lag_table.shape, bf16),
            pltpu.VMEM(left_tones.shape, bf16),
            pltpu.VMEM(flat.shape, bf16),
            pltpu.VMEM(near.shape, bf16),
            pltpu.VMEM(far.shape, bf16),
            pltpu.VMEM((2 * BINS, SEGMENTS * CHANNELS), bf16),
            pltpu.VMEM((TONES, SEGMENTS * 16, 2 * CHANNELS), bf16),
            pltpu.VMEM((4, CHANNELS // 16, TONES // 2 * 8, 256), bf16),
            pltpu.VMEM((CHANNELS, CHANNELS), jnp.float32),
            pltpu.VMEM((2, LAGS, 16, CHANNELS), bf16),
            pltpu.SemaphoreType.DMA((5,)),
            pltpu.SemaphoreType.DMA((PARTS,)),
            pltpu.SemaphoreType.DMA((2,)),
        ],
        compiler_params=pltpu.CompilerParams(vmem_limit_bytes=56 * 2**20),
    )(right_table, lag_table, left_tones, flat, near, far)


def per_device(spectra, plan):
    left_table, right_table = (jnp.asarray(table, jnp.bfloat16) for table in window_tables())
    lag_table = jnp.asarray(lag_tables(), jnp.bfloat16)
    left_tones, flat, near, far = ring_move(plan, spectra.reshape(ROWS, BINS), left_table)
    return correlate(left_tones, flat, near, far, right_table, lag_table)[None, None]


def solution(mesh):
    in_specs = (P("ch", "seg", None, None, None), P(None, "ch"))
    out_specs = P("ch", "seg", None, None, None)
    return jax.shard_map(
        per_device, mesh=mesh, in_specs=in_specs, out_specs=out_specs, check_vma=False
    )
```
